128 devices in a mesh: brow: 8 (over x_hi, z), bcol: 16 (over y, x_lo, core).
Axes of the slice: x: 4 (x_hi: 2, x_lo: 2; x = x_hi * 2 + x_lo), y: 4, z: 4, core: 2. Of those that a mesh axis runs over, the one named last changes fastest.
Arguments:
- x_start: float32 [131072, 32], P(('brow', 'bcol')), may hold values from -6 to 6
- bin_mask: int32 [131072], P(('brow', 'bcol')), may hold values 0 or 1
- band: bfloat16 [512, 16, 256, 256], P('brow', 'bcol'), may hold values from -0.0625 to 0.0625
- off_tiles: bfloat16 [8, 16, 64, 256, 256], P('brow', 'bcol'), may hold values from -0.0625 to 0.0625
- off_rows: int32 [8, 16, 64], P('brow', 'bcol'), may hold values from 0 to 63
- off_cols: int32 [8, 16, 64], P('brow', 'bcol'), may hold values from 0 to 31
- off_count: int32 [8, 16], P('brow', 'bcol'), may hold values from 32 to 64, as said below
Outputs:
- eigen_block: float32 [131072, 32], P(('brow', 'bcol'))
- ritz_matrix: float32 [32, 32], replicated
The draws below stay inside these ranges and needn't reach their ends.
Inputs may be any that keep to these rules, and one draw needn't show every extreme that they name: `off_count`: slots at and beyond a device's count hold no tile; some device uses all 64 slots; coordinates on a device may repeat.
All inputs are finite; a program needn't handle non-finite values. No bound on the sum of `bin_mask` on one device may be relied on, other than what follows from the above.
Results may differ from the reference program's by a relative error of at most 0.0026.
Values may be sent and summed in bfloat16 or wider, within the bound.
No kernel may reach another device: no remote copies, remote signals or barrier semaphores. Data moves between devices by JAX's collectives and lax.ppermute only.
A program may use at most 128 MiB of HBM per device.

```python
import jax
import jax.numpy as jnp
from jax import lax

TILE = 256
VECTORS = 32
SLAB_TILES = 4
OFF_DEV = 64
STEPS = 3
ROW_TILES = 64
COL_TILES = 32
ALL_TILES = 512
BINS = 131072
BANDS = 16
N_BROW = 8
N_BCOL = 16


def draw_off_count(key, part):
    key = jax.random.fold_in(key, 7)
    counts = jax.random.randint(key, (N_BROW, N_BCOL), OFF_DEV // 2, OFF_DEV + 1)
    return counts.at[0, 0].set(OFF_DEV).astype(jnp.int32)


def place_ends(drawn, own_key, smallest, largest):
    longest = drawn.shape.index(max(drawn.shape))
    spots = []
    for shift in (0, 1):
        where = [jax.random.randint(jax.random.fold_in(own_key, axis), (), 0, length) for axis, length in enumerate(drawn.shape)]
        where[longest] = (where[longest] + shift) % drawn.shape[longest]
        spots.append(tuple(where))
    return drawn.at[spots[0]].set(smallest).at[spots[1]].set(largest)


def levels(key, dims, shards, least, largest):
    loudness = 1.0
    for position, parts in shards:
        heights = jax.random.uniform(jax.random.fold_in(jax.random.fold_in(key, 6), position), (parts,), jnp.float32, least / len(shards), largest / len(shards))
        loudness = loudness * jnp.repeat(jnp.exp(heights), dims[position] // parts).reshape((-1,) + (1,) * (len(dims) - 1 - position))
    return loudness


def scatter_about(key, extent, scale, limit, cuts=(), kind=jnp.bfloat16):
    loudness = levels(key, extent, cuts, -0.22, 0.18) if cuts else 1.0
    drawn = jax.random.normal(key, extent, jnp.float32) * scale * loudness
    return jnp.minimum(jnp.maximum(drawn, -limit), limit).astype(kind)


def setup_inputs(seed: int = 0) -> dict:
    arg_keys = jax.random.split(jax.random.key(seed), 8)
    return {
        "x_start": scatter_about(arg_keys[0], (BINS, VECTORS), 1.0, 6.0, ((0, 128),), jnp.float32),
        "bin_mask": place_ends((jax.random.randint(arg_keys[1], (BINS,), 0, 16) < 15).astype(jnp.int32), jax.random.fold_in(arg_keys[1], 1), 0, 1),
        "band": scatter_about(arg_keys[2], (ALL_TILES, BANDS, TILE, TILE), (2 * BANDS * TILE) ** -0.5, 0.0625, ((0, 8), (1, 16))),
        "off_tiles": scatter_about(arg_keys[3], (N_BROW, N_BCOL, OFF_DEV, TILE, TILE), (2 * BANDS * TILE) ** -0.5, 0.0625, ((0, 8), (1, 16))),
        "off_rows": place_ends(jax.random.randint(arg_keys[4], (N_BROW, N_BCOL, OFF_DEV), 0, ROW_TILES), jax.random.fold_in(arg_keys[4], 1), 0, ROW_TILES - 1).astype(jnp.int32),
        "off_cols": place_ends(jax.random.randint(arg_keys[5], (N_BROW, N_BCOL, OFF_DEV), 0, COL_TILES), jax.random.fold_in(arg_keys[5], 1), 0, COL_TILES - 1).astype(jnp.int32),
        "off_count": draw_off_count(jax.random.fold_in(arg_keys[7], 71), 0),
    }


PRECISE = lax.Precision.HIGHEST
EPSILON = 1e-06

def gram_of(left, right):
    return jnp.dot(left.T.astype(jnp.float32), right.astype(jnp.float32), precision=PRECISE, preferred_element_type=jnp.float32)

def symmetric(matrix):
    return 0.5 * (matrix + matrix.T)

def right_solve(values, factor):
    return lax.linalg.triangular_solve(factor, values, left_side=False, lower=True, transpose_a=True)

def left_solve(factor, values, transposed):
    return lax.linalg.triangular_solve(factor, values, left_side=True, lower=True, transpose_a=transposed)

def projected(factor, matrix):
    return symmetric(right_solve(left_solve(factor, matrix, False), factor))

def rayleigh_ritz(basis_gram, image_gram, block_width):
    factor = jnp.linalg.cholesky(basis_gram)
    reduced = projected(factor, image_gram)
    basis_order = reduced.shape[0]
    scaling = jnp.sqrt(jnp.sum(reduced * reduced))
    filtered = (reduced + scaling * jnp.eye(basis_order, dtype=jnp.float32)) / (2.0 * scaling)
    filtered = jnp.dot(filtered, filtered, precision=PRECISE)
    filtered = jnp.dot(filtered, filtered, precision=PRECISE)
    leading = filtered[:, :block_width]
    small_factor = jnp.linalg.cholesky(gram_of(leading, leading))
    orthonormal = right_solve(leading, small_factor)
    return left_solve(factor, orthonormal, True)

def apply_matrix(vectors, mask_float, band, off_tiles, off_rows, off_cols, off_count):
    block_width = vectors.shape[1]
    packed = (vectors * mask_float[:, None]).astype(jnp.bfloat16).astype(jnp.float32)
    packed = packed.reshape(ALL_TILES, TILE, block_width)
    extended = jnp.concatenate([packed, jnp.zeros((BANDS, TILE, block_width), jnp.float32)], axis=0)
    spread = jnp.zeros((ALL_TILES + BANDS, TILE, block_width), jnp.float32)
    for offset in range(BANDS):
        blocks = band[:, offset].astype(jnp.float32)
        spread = spread.at[:ALL_TILES].add(jnp.einsum('nab,nbk->nak', blocks, extended[offset:offset + ALL_TILES], precision=PRECISE))
        spread = spread.at[offset:offset + ALL_TILES].add(jnp.einsum('nba,nbk->nak', blocks, packed, precision=PRECISE))
    totals = spread[:ALL_TILES]
    rows_global = (jnp.arange(N_BROW, dtype=jnp.int32)[:, None, None] * ROW_TILES + off_rows).reshape(-1, OFF_DEV)
    col_owner = jnp.arange(N_BCOL, dtype=jnp.int32)[None, :, None]
    cols_global = ((off_cols // SLAB_TILES * N_BCOL + col_owner) * SLAB_TILES + off_cols % SLAB_TILES).reshape(-1, OFF_DEV)
    live_slots = (jnp.arange(OFF_DEV, dtype=jnp.int32)[None, None, :] < off_count[:, :, None]).astype(jnp.float32)
    live_slots = live_slots.reshape(-1, OFF_DEV)
    tiles_all = off_tiles.reshape(-1, OFF_DEV, TILE, TILE)

    def visit(carry, device_item):
        tiles, row_ids, col_ids, live = device_item
        tiles = tiles.astype(jnp.float32)
        forward = jnp.einsum('sab,sbk->sak', tiles, packed[col_ids], precision=PRECISE) * live[:, None, None]
        returned = jnp.einsum('sba,sbk->sak', tiles, packed[row_ids], precision=PRECISE) * live[:, None, None]
        carry = carry.at[row_ids].add(forward)
        carry = carry.at[col_ids].add(returned)
        return (carry, None)
    totals, _ = lax.scan(visit, totals, (tiles_all, rows_global, cols_global, live_slots))
    return totals.reshape(BINS, block_width) * mask_float[:, None]

def reference(x_start, bin_mask, band, off_tiles, off_rows, off_cols, off_count):
    mask_float = bin_mask.astype(jnp.float32)

    def apply_operator(vectors):
        return apply_matrix(vectors, mask_float, band, off_tiles, off_rows, off_cols, off_count)
    block_width = x_start.shape[1]
    started = x_start * mask_float[:, None]
    first_image = apply_operator(started)
    factor = jnp.linalg.cholesky(gram_of(started, started))
    vectors = right_solve(started, factor)
    images_now = right_solve(first_image, factor)
    previous = ()
    for iteration in range(STEPS):
        ritz_now = symmetric(gram_of(vectors, images_now))
        residual = images_now - jnp.dot(vectors, ritz_now, precision=PRECISE)
        residual_image = apply_operator(residual)
        tail_cols = jnp.concatenate([residual] + list(previous[:1]), axis=1)
        tail_images = jnp.concatenate([residual_image] + list(previous[1:]), axis=1)
        col_norms = lax.optimization_barrier(jnp.sum(tail_cols * tail_cols, axis=0))
        scaling = lax.rsqrt(col_norms + EPSILON)
        basis_cols = jnp.concatenate([vectors, tail_cols * scaling[None, :]], axis=1)
        image_cols = jnp.concatenate([images_now, tail_images * scaling[None, :]], axis=1)
        basis_gram = gram_of(basis_cols, basis_cols)
        image_gram = symmetric(gram_of(basis_cols, image_cols))
        weights = rayleigh_ritz(basis_gram, image_gram, block_width)
        vectors = jnp.dot(basis_cols, weights, precision=PRECISE)
        images_now = jnp.dot(image_cols, weights, precision=PRECISE)
        previous = (jnp.dot(basis_cols[:, block_width:], weights[block_width:], precision=PRECISE), jnp.dot(image_cols[:, block_width:], weights[block_width:], precision=PRECISE))
    ritz_final = symmetric(gram_of(vectors, images_now))
    return (vectors, ritz_final)
```

```python
import functools

import jax
import jax.numpy as jnp
from jax import lax
from jax.experimental import pallas as pl
from jax.experimental.pallas import tpu as pltpu
from jax.sharding import PartitionSpec as P

STEPS = 3
PRECISE = lax.Precision.HIGHEST
EPSILON = 1e-06
F32 = jnp.float32
BF16 = jnp.bfloat16
GROUP = 8
VMEM_BYTES = 40 * 1024 * 1024


def flip(value, axis, by):
    length = lax.axis_size(axis)
    return lax.ppermute(value, axis, [(i, i ^ by) for i in range(length)])


def flip_both(value, row_by, col_by):
    rows, cols = lax.axis_size("brow"), lax.axis_size("bcol")
    pairs = [
        (r * cols + c, (r ^ row_by) * cols + (c ^ col_by)) for r in range(rows) for c in range(cols)
    ]
    return lax.ppermute(value, ("brow", "bcol"), pairs)


def shifted(value, axis, by):
    length = lax.axis_size(axis)
    pairs = [(i, i + by) for i in range(length) if 0 <= i + by < length]
    return lax.ppermute(value, axis, pairs)


def sum_all(value):
    value = value + flip(value, "bcol", 1)
    value = (value + flip(value, "bcol", 4)) + (flip(value, "bcol", 8) + flip(value, "bcol", 12))
    value = (value + flip(value, "brow", 1)) + (flip(value, "brow", 2) + flip(value, "brow", 3))
    value = (value + flip(value, "bcol", 2)) + (flip(value, "brow", 4) + flip_both(value, 4, 2))
    return value


def whole(shape):
    return pl.BlockSpec(shape, lambda *_: (0,) * len(shape))


def params():
    return pltpu.CompilerParams(vmem_limit_bytes=VMEM_BYTES)


def assemble_kernel(ids, p0, p1, p2, p3, q0, q1, q2, q3, rows_out, rim_out):
    me = ids[1]
    for s in range(16):
        slot = me ^ s
        core, half, quarter = slot & 1, (slot >> 1) & 1, slot >> 2
        for k in range(4):
            for parity, ref in ((0, (p0, p1, p2, p3)[k]), (1, (q0, q1, q2, q3)[k])):

                @pl.when((quarter == k) & (core == parity))
                def _():
                    rows_out[4 * s : 4 * s + 4] = ref[half]
                    if s < 4:
                        rim_out[4 * s : 4 * s + 4] = ref[half]


def assemble(ids, parts):
    return pl.pallas_call(
        assemble_kernel,
        grid_spec=pltpu.PrefetchScalarGridSpec(
            num_scalar_prefetch=1,
            grid=(1,),
            in_specs=[whole((2, 4, 32, 256))] * 8,
            out_specs=[whole((64, 32, 256)), whole((16, 32, 256))],
        ),
        out_shape=[
            jax.ShapeDtypeStruct((64, 32, 256), BF16),
            jax.ShapeDtypeStruct((16, 32, 256), BF16),
        ],
        compiler_params=params(),
        cost_estimate=pl.CostEstimate(flops=0, bytes_accessed=2 << 20, transcendentals=0),
    )(ids, *parts)


def back_kernel(ids, band, rows, spread, spill):
    me = ids[1]
    step = pl.program_id(0)

    @pl.when(step == 0)
    def _():
        for d in range(15):

            @pl.when(d < me)
            def _():
                spread[d] = jnp.zeros((32, 256), F32)

            @pl.when(d >= me)
            def _():
                spill[d] = jnp.zeros((32, 256), F32)

        spill[15] = jnp.zeros((32, 256), F32)

    for g in range(GROUP):
        i = step * GROUP + g
        value = jnp.dot(rows[i], band[g], preferred_element_type=F32)
        target = i + me

        @pl.when(target < 64)
        def _():
            spread[jnp.minimum(target, 63)] = value

        @pl.when(target >= 64)
        def _():
            spill[jnp.maximum(target - 64, 0)] = value


def band_back(ids, band, rows):
    return pl.pallas_call(
        back_kernel,
        grid_spec=pltpu.PrefetchScalarGridSpec(
            num_scalar_prefetch=1,
            grid=(64 // GROUP,),
            in_specs=[
                pl.BlockSpec((GROUP, 256, 256), lambda i, *_: (i, 0, 0)),
                whole((64, 32, 256)),
            ],
            out_specs=[whole((64, 32, 256)), whole((16, 32, 256))],
        ),
        out_shape=[
            jax.ShapeDtypeStruct((64, 32, 256), F32),
            jax.ShapeDtypeStruct((16, 32, 256), F32),
        ],
        compiler_params=params(),
        cost_estimate=pl.CostEstimate(
            flops=2 * 64 * 256 * 256 * 32, bytes_accessed=11 << 20, transcendentals=0
        ),
    )(ids, band, rows)


def far_kernel(ids, row_ids, col_ids, tiles, rows, base, c0, c1, c2, c3, out, k0, k1, k2, k3, cols, acc):
    mine, count = ids[0], ids[2]
    step = pl.program_id(0)

    @pl.when(step == 0)
    def _():
        out[...] = base[...]
        acc[...] = jnp.zeros_like(acc)
        for s in range(8):
            slot = mine ^ s
            for k, ref in enumerate((c0, c1, c2, c3)):

                @pl.when((slot & 3) == k)
                def _():
                    cols[4 * s : 4 * s + 4] = ref[slot >> 2]

    def both(g, i):
        a, b = row_ids[i], col_ids[i]
        forward = lax.dot_general(
            cols[b], tiles[g], (((1,), (1,)), ((), ())), preferred_element_type=F32
        )
        back = jnp.dot(rows[a], tiles[g], preferred_element_type=F32)
        return a, b, forward, back

    first = step * GROUP

    @pl.when(first + GROUP <= count)
    def _():
        found = [both(g, first + g) for g in range(GROUP)]
        for a, b, forward, back in found:
            out[a] += forward
            acc[b] += back

    @pl.when((first + GROUP > count) & (first < count))
    def _():
        for g in range(GROUP):

            @pl.when(first + g < count)
            def _():
                a, b, forward, back = both(g, first + g)
                out[a] += forward
                acc[b] += back

    @pl.when(step == pl.num_programs(0) - 1)
    def _():
        for j in range(8):
            source = mine ^ j
            (k0, k1, k2, k3)[j & 3][j >> 2] = acc[pl.ds(4 * source, 4)]


def far(ids, row_ids, col_ids, tiles, rows, base, parts):
    pair = (2, 4, 32, 256)
    return pl.pallas_call(
        far_kernel,
        grid_spec=pltpu.PrefetchScalarGridSpec(
            num_scalar_prefetch=3,
            grid=(64 // GROUP,),
            in_specs=[
                pl.BlockSpec((GROUP, 256, 256), lambda i, *_: (i, 0, 0)),
                whole((64, 32, 256)),
                whole((64, 32, 256)),
            ]
            + [whole(pair)] * 4,
            out_specs=[whole((64, 32, 256))] + [whole(pair)] * 4,
            scratch_shapes=[pltpu.VMEM((32, 32, 256), BF16), pltpu.VMEM((32, 32, 256), F32)],
        ),
        out_shape=[jax.ShapeDtypeStruct((64, 32, 256), F32)] + [jax.ShapeDtypeStruct(pair, F32)] * 4,
        compiler_params=params(),
        cost_estimate=pl.CostEstimate(
            flops=4 * 64 * 256 * 256 * 32, bytes_accessed=15 << 20, transcendentals=0
        ),
    )(ids, row_ids, col_ids, tiles, rows, base, *parts)


def forward_kernel(ids, band, rows, rim, base, spilled, same, other, extended):
    me = ids[1]
    step = pl.program_id(0)

    @pl.when(step == 0)
    def _():
        extended[:64] = rows[...]
        extended[64:80] = rim[...]

    for h in range(GROUP // 4):
        slab = step * (GROUP // 4) + h
        slot = me ^ slab
        total = []
        for t in range(4):
            i = slab * 4 + t
            product = lax.dot_general(
                extended[i + me], band[4 * h + t], (((1,), (1,)), ((), ())), preferred_element_type=F32
            )
            extra = jnp.where(i < 16, spilled[jnp.minimum(i, 15)], 0.0)
            total.append(product + base[i] + extra)

        @pl.when((slot & 1) == 0)
        def _():
            for t in range(4):
                same[slot >> 1, t] = total[t]

        @pl.when((slot & 1) == 1)
        def _():
            for t in range(4):
                other[slot >> 1, t] = total[t]


def band_forward(ids, band, rows, rim, base, spilled):
    return pl.pallas_call(
        forward_kernel,
        grid_spec=pltpu.PrefetchScalarGridSpec(
            num_scalar_prefetch=1,
            grid=(64 // GROUP,),
            in_specs=[
                pl.BlockSpec((GROUP, 256, 256), lambda i, *_: (i, 0, 0)),
                whole((64, 32, 256)),
                whole((16, 32, 256)),
                whole((64, 32, 256)),
                whole((16, 32, 256)),
            ],
            out_specs=[whole((8, 4, 32, 256))] * 2,
            scratch_shapes=[pltpu.VMEM((80, 32, 256), BF16)],
        ),
        out_shape=[jax.ShapeDtypeStruct((8, 4, 32, 256), F32)] * 2,
        compiler_params=params(),
        cost_estimate=pl.CostEstimate(
            flops=2 * 64 * 256 * 256 * 32, bytes_accessed=14 << 20, transcendentals=0
        ),
    )(ids, band, rows, rim, base, spilled)


def fold_kernel(same, arrived, *outs):
    for k in range(4):
        outs[k][...] = same[2 * k : 2 * k + 2] + arrived[2 * k : 2 * k + 2]


def fold(same, arrived):
    pair = jax.ShapeDtypeStruct((2, 4, 32, 256), F32)
    return pl.pallas_call(
        fold_kernel,
        out_shape=[pair] * 4,
        compiler_params=params(),
        cost_estimate=pl.CostEstimate(flops=0, bytes_accessed=3 << 20, transcendentals=0),
    )(same, arrived)


def against(left, right):
    return lax.dot_general(
        left, right, (((1,), (1,)), ((), ())), precision=PRECISE, preferred_element_type=F32
    )


def gram_kernel(n, with_images, *refs):
    basis, images = refs[: n + 1], refs[n + 1 : 2 * n + 1]
    terms = refs[2 * n + 1 : 2 * n + 5]
    mask, image_out, gram_out = refs[2 * n + 5 :]
    plain = jnp.zeros((32, 32 * (n + 1)), F32)
    cross = jnp.zeros((32, 32 * (n + 1)), F32)
    for t in range(4):
        image = ((terms[0][t] + terms[1][t]) + (terms[2][t] + terms[3][t])) * mask[t]
        image_out[t] = image
        newest = basis[-1][t]
        columns = jnp.concatenate([b[t] for b in basis], axis=0)
        plain += against(newest, columns)
        seen = jnp.concatenate([b[t] for b in images] + [image], axis=0)
        cross += 0.5 * (against(newest, seen) + against(image, columns))
    gram_out[...] = jnp.concatenate([plain, cross], axis=1)


def grams(older, older_images, newest, terms, mask):
    n = len(older)
    return pl.pallas_call(
        functools.partial(gram_kernel, n, True),
        out_shape=[
            jax.ShapeDtypeStruct((4, 32, 256), F32),
            jax.ShapeDtypeStruct((32, 64 * (n + 1)), F32),
        ],
        compiler_params=params(),
        cost_estimate=pl.CostEstimate(flops=1 << 27, bytes_accessed=1 << 20, transcendentals=0),
    )(*older, newest, *older_images, *terms, mask)


def mul(left, right):
    return jnp.dot(left, right, precision=PRECISE, preferred_element_type=F32)


def update_kernel(n, last, *refs):
    basis, images = refs[:n], refs[n : 2 * n]
    weights, ritz, mask = refs[2 * n : 2 * n + 3]
    outs = refs[2 * n + 3 :]
    for t in range(4):
        moved = mul(weights[...], jnp.concatenate([b[t] for b in basis], axis=0))
        outs[0][t] = moved[:32]
        if last:
            continue
        moved_images = mul(weights[...], jnp.concatenate([b[t] for b in images], axis=0))
        outs[1][t] = moved_images[:32]
        residual = moved_images[:32] - mul(ritz[...], moved[:32])
        outs[2][t] = residual
        outs[3][t] = (residual * mask[t]).astype(BF16)
        if moved.shape[0] > 32:
            outs[4][t] = moved[32:]
            outs[5][t] = moved_images[32:]


def update(basis, images, weights, ritz, mask, last=False):
    n = len(basis)
    slab = jax.ShapeDtypeStruct((4, 32, 256), F32)
    outs = [slab] if last else [slab, slab, slab, jax.ShapeDtypeStruct((4, 32, 256), BF16)]
    if not last and weights.shape[0] > 32:
        outs += [slab, slab]
    return pl.pallas_call(
        functools.partial(update_kernel, n, last),
        out_shape=outs,
        compiler_params=params(),
        cost_estimate=pl.CostEstimate(flops=1 << 27, bytes_accessed=1 << 20, transcendentals=0),
    )(*basis, *images, weights, ritz, mask)


def symmetric(matrix):
    return 0.5 * (matrix + matrix.T)


def right_solve(values, factor):
    return lax.linalg.triangular_solve(
        factor, values, left_side=False, lower=True, transpose_a=True
    )


def left_solve(factor, values, transposed):
    return lax.linalg.triangular_solve(
        factor, values, left_side=True, lower=True, transpose_a=transposed
    )


def rayleigh_ritz(basis_gram, image_gram, block_width):
    factor = jnp.linalg.cholesky(basis_gram)
    reduced = symmetric(right_solve(left_solve(factor, image_gram, False), factor))
    order = reduced.shape[0]
    scaling = jnp.sqrt(jnp.sum(reduced * reduced))
    filtered = (reduced + scaling * jnp.eye(order, dtype=F32)) / (2.0 * scaling)
    filtered = mul(filtered, filtered)
    filtered = mul(filtered, filtered)
    leading = filtered[:, :block_width]
    small_factor = jnp.linalg.cholesky(mul(leading.T, leading))
    orthonormal = right_solve(leading, small_factor)
    return left_solve(factor, orthonormal, True)


def grown(known, row):
    edge = row[:, : known.shape[0]]
    return jnp.concatenate(
        [
            jnp.concatenate([known, edge.T], axis=1),
            jnp.concatenate([edge, symmetric(row[:, known.shape[0] :])], axis=1),
        ],
        axis=0,
    )


def body(x_start, bin_mask, band, off_tiles, off_rows, off_cols, off_count):
    width = x_start.shape[1]
    band = band[:, 0]
    tiles = off_tiles[0, 0]
    row_ids, col_ids = off_rows[0, 0], off_cols[0, 0]
    ids = jnp.stack(
        [lax.axis_index("brow"), lax.axis_index("bcol"), off_count[0, 0], jnp.int32(0)]
    ).astype(jnp.int32)
    mask = bin_mask.astype(F32).reshape(4, 1, 256)
    started = x_start.T.reshape(width, 4, 256).transpose(1, 0, 2) * mask

    def apply_operator(packed):
        pair = jnp.stack([packed, flip(packed, "bcol", 2)])
        near = [pair] + [flip(pair, "bcol", 4 * k) for k in (1, 2, 3)]
        across = [flip(part, "bcol", 1) for part in near]
        col_pair = jnp.stack([packed, flip(packed, "brow", 4)])
        col_parts = [col_pair] + [flip(col_pair, "brow", k) for k in (1, 2, 3)]
        rows, rim = assemble(ids, near + across)
        rim = shifted(rim, "brow", -1)
        spread, spill = band_back(ids, band, rows)
        spilled = shifted(spill, "brow", 1)
        base, *col_sums = far(ids, row_ids, col_ids, tiles, rows, spread, col_parts)
        c0, c1, c2, c3 = [col_sums[0]] + [flip(col_sums[k], "brow", k) for k in (1, 2, 3)]
        col_total = (c0 + c1) + (c2 + c3)
        col_other = flip(col_total[1], "brow", 4)
        same, other = band_forward(ids, band, rows, rim, base, spilled)
        folded = fold(same, flip(other, "bcol", 1))
        r0, r1, r2, r3 = [folded[0]] + [flip(folded[k], "bcol", 4 * k) for k in (1, 2, 3)]
        row_total = (r0 + r1) + (r2 + r3)
        row_other = flip(row_total[1], "bcol", 2)
        return [row_total[0], row_other, col_total[0], col_other]

    terms = apply_operator((started * mask).astype(BF16))
    image, gram = grams([], [], started, terms, mask)
    gram = sum_all(gram)
    start_gram, start_images = symmetric(gram[:, :width]), symmetric(gram[:, width:])
    factor = jnp.linalg.cholesky(start_gram)
    inverse = left_solve(factor, jnp.eye(width, dtype=F32), False)
    ritz = symmetric(mul(mul(inverse, start_images), inverse.T))
    known_basis, known_images = symmetric(mul(mul(inverse, start_gram), inverse.T)), ritz
    vectors, images, residual, packed = update([started], [image], inverse, ritz, mask)
    older, older_images = [vectors], [images]
    for step in range(STEPS):
        terms = apply_operator(packed)
        residual_image, gram = grams(older, older_images, residual, terms, mask)
        gram = sum_all(gram)
        order = width * (len(older) + 1)
        basis_gram = grown(known_basis, gram[:, :order])
        image_gram = grown(known_images, gram[:, order:])
        scaling = lax.rsqrt(jnp.diagonal(basis_gram)[width:] + EPSILON)
        scaling = jnp.concatenate([jnp.ones((width,), F32), scaling])
        weights = scaling[:, None] * rayleigh_ritz(
            scaling[:, None] * basis_gram * scaling[None, :],
            scaling[:, None] * image_gram * scaling[None, :],
            width,
        )
        tail = jnp.concatenate([jnp.zeros((width, width), F32), weights[width:]], axis=0)
        both = jnp.concatenate([weights, tail], axis=1)
        known_images = symmetric(mul(both.T, mul(image_gram, both)))
        ritz = known_images[:width, :width]
        basis, basis_images = older + [residual], older_images + [residual_image]
        if step == STEPS - 1:
            (vectors,) = update(basis, basis_images, weights.T, ritz, mask, last=True)
        else:
            known_basis = symmetric(mul(both.T, mul(basis_gram, both)))
            vectors, images, residual, packed, previous, previous_images = update(
                basis, basis_images, both.T, ritz, mask
            )
            older, older_images = [vectors, previous], [images, previous_images]
    return vectors.transpose(1, 0, 2).reshape(width, -1).T, ritz


def solution(mesh):
    return jax.shard_map(
        body,
        mesh=mesh,
        in_specs=(
            P(("brow", "bcol"), None),
            P(("brow", "bcol")),
            P("brow", "bcol", None, None),
            P("brow", "bcol", None, None, None),
            P("brow", "bcol", None),
            P("brow", "bcol", None),
            P("brow", "bcol"),
        ),
        out_specs=(P(("brow", "bcol"), None), P()),
        check_vma=False,
    )
```

```python
import functools

import jax
import jax.numpy as jnp
from jax import lax
from jax.experimental import pallas as pl
from jax.experimental.pallas import tpu as pltpu
from jax.sharding import PartitionSpec as P

STEPS = 3
PRECISE = lax.Precision.HIGHEST
EPSILON = 1e-06
F32 = jnp.float32
BF16 = jnp.bfloat16
GROUP = 16
VMEM_BYTES = 40 * 1024 * 1024


def flip(value, axis, by):
    length = lax.axis_size(axis)
    return lax.ppermute(value, axis, [(i, i ^ by) for i in range(length)])


def flip_both(value, row_by, col_by):
    rows, cols = lax.axis_size("brow"), lax.axis_size("bcol")
    pairs = [
        (r * cols + c, (r ^ row_by) * cols + (c ^ col_by)) for r in range(rows) for c in range(cols)
    ]
    return lax.ppermute(value, ("brow", "bcol"), pairs)


def shifted(value, axis, by):
    length = lax.axis_size(axis)
    pairs = [(i, i + by) for i in range(length) if 0 <= i + by < length]
    return lax.ppermute(value, axis, pairs)


def sum_all(value):
    value = value + flip(value, "bcol", 1)
    value = (value + flip(value, "bcol", 4)) + (flip(value, "bcol", 8) + flip(value, "bcol", 12))
    value = (value + flip(value, "brow", 1)) + (flip(value, "brow", 2) + flip(value, "brow", 3))
    value = (value + flip(value, "bcol", 2)) + (flip(value, "brow", 4) + flip_both(value, 4, 2))
    return value


def whole(shape):
    return pl.BlockSpec(shape, lambda *_: (0,) * len(shape))


def params():
    return pltpu.CompilerParams(vmem_limit_bytes=VMEM_BYTES)


def assemble_kernel(ids, p0, p1, p2, p3, q0, q1, q2, q3, c0, c1, c2, c3, rows_out, rim_out, cols_out):
    mine, me = ids[0], ids[1]
    near, across, along = (p0, p1, p2, p3), (q0, q1, q2, q3), (c0, c1, c2, c3)
    for k in range(4):
        for half in range(2):
            for parity, refs in ((0, near), (1, across)):
                slab = me ^ (4 * k + 2 * half + parity)
                rows_out[pl.ds(4 * slab, 4)] = refs[k][half]
            slab = mine ^ (4 * half + k)
            cols_out[pl.ds(4 * slab, 4)] = along[k][half]
    rim_out[...] = rows_out[:16]


def assemble(ids, parts):
    return pl.pallas_call(
        assemble_kernel,
        grid_spec=pltpu.PrefetchScalarGridSpec(
            num_scalar_prefetch=1,
            grid=(1,),
            in_specs=[whole((2, 4, 32, 256))] * 12,
            out_specs=[whole((64, 32, 256)), whole((16, 32, 256)), whole((32, 32, 256))],
        ),
        out_shape=[
            jax.ShapeDtypeStruct((64, 32, 256), BF16),
            jax.ShapeDtypeStruct((16, 32, 256), BF16),
            jax.ShapeDtypeStruct((32, 32, 256), BF16),
        ],
        compiler_params=params(),
        cost_estimate=pl.CostEstimate(flops=0, bytes_accessed=3 << 20, transcendentals=0),
    )(ids, *parts)


def back_kernel(ids, band, rows, spread, spill):
    me = ids[1]
    step = pl.program_id(0)

    @pl.when(step == 0)
    def _():
        spread[:16] = jnp.zeros((16, 32, 256), F32)
        spread[64:] = jnp.zeros((16, 32, 256), F32)

    first = step * GROUP
    products = [
        jnp.dot(rows[first + g], band[g], preferred_element_type=F32) for g in range(GROUP)
    ]
    for g in range(GROUP):
        spread[first + g + me] = products[g]

    @pl.when(step == pl.num_programs(0) - 1)
    def _():
        spill[...] = spread[64:].astype(BF16)


def band_back(ids, band, rows):
    return pl.pallas_call(
        back_kernel,
        grid_spec=pltpu.PrefetchScalarGridSpec(
            num_scalar_prefetch=1,
            grid=(64 // GROUP,),
            in_specs=[
                pl.BlockSpec((GROUP, 256, 256), lambda i, *_: (i, 0, 0)),
                whole((64, 32, 256)),
            ],
            out_specs=[whole((80, 32, 256)), whole((16, 32, 256))],
        ),
        out_shape=[
            jax.ShapeDtypeStruct((80, 32, 256), F32),
            jax.ShapeDtypeStruct((16, 32, 256), BF16),
        ],
        compiler_params=params(),
        cost_estimate=pl.CostEstimate(
            flops=2 * 64 * 256 * 256 * 32, bytes_accessed=11 << 20, transcendentals=0
        ),
    )(ids, band, rows)


def far_kernel(ids, row_ids, col_ids, tiles, rows, cols, base, out, k0, k1, k2, k3, acc):
    mine, count = ids[0], ids[2]
    step = pl.program_id(0)

    @pl.when(step == 0)
    def _():
        out[...] = base[...]
        acc[...] = jnp.zeros_like(acc)

    def visit(base_slot, partial):
        first = step * GROUP + base_slot
        found = []
        for g in range(8):
            i = first + g
            live = i < count
            a, b = row_ids[i], col_ids[i]
            if partial:
                a, b = jnp.where(live, a, 0), jnp.where(live, b, 0)
            tile = tiles[base_slot + g]
            forward = lax.dot_general(
                cols[b], tile, (((1,), (1,)), ((), ())), preferred_element_type=F32
            )
            back = jnp.dot(rows[a], tile, preferred_element_type=F32)
            if partial:
                forward, back = jnp.where(live, forward, 0.0), jnp.where(live, back, 0.0)
            found.append((a, b, forward, back))
        for a, b, forward, back in found:
            out[a] += forward
            acc[b] += back

    for h in range(0, GROUP, 8):
        first = step * GROUP + h

        @pl.when(first + 8 <= count)
        def _():
            visit(h, False)

        @pl.when((first + 8 > count) & (first < count))
        def _():
            visit(h, True)

    @pl.when(step == pl.num_programs(0) - 1)
    def _():
        for j in range(8):
            piece = acc[pl.ds(4 * (mine ^ j), 4)]
            target = (k0, k1, k2, k3)[j & 3]
            target[j >> 2] = piece.astype(target.dtype)


PAIR = (2, 4, 32, 256)


def pair_shapes():
    return [jax.ShapeDtypeStruct(PAIR, F32)] + [jax.ShapeDtypeStruct(PAIR, BF16)] * 3


def far(ids, row_ids, col_ids, tiles, rows, cols, base):
    return pl.pallas_call(
        far_kernel,
        grid_spec=pltpu.PrefetchScalarGridSpec(
            num_scalar_prefetch=3,
            grid=(64 // GROUP,),
            in_specs=[
                pl.BlockSpec((GROUP, 256, 256), lambda i, *_: (i, 0, 0)),
                whole((64, 32, 256)),
                whole((32, 32, 256)),
                whole((64, 32, 256)),
            ],
            out_specs=[whole((64, 32, 256))] + [whole(PAIR)] * 4,
            scratch_shapes=[pltpu.VMEM((32, 32, 256), F32)],
        ),
        out_shape=[jax.ShapeDtypeStruct((64, 32, 256), F32)] + pair_shapes(),
        compiler_params=params(),
        cost_estimate=pl.CostEstimate(
            flops=4 * 64 * 256 * 256 * 32, bytes_accessed=15 << 20, transcendentals=0
        ),
    )(ids, row_ids, col_ids, tiles, rows, cols, base)


def forward_kernel(ids, band, rows, rim, base, spilled, halves, extended):
    me = ids[1]
    step = pl.program_id(0)

    @pl.when(step == 0)
    def _():
        extended[:64] = rows[...]
        extended[64:80] = rim[...]

    first = step * GROUP
    products = [
        lax.dot_general(
            extended[first + g + me], band[g], (((1,), (1,)), ((), ())), preferred_element_type=F32
        )
        + base[first + g]
        for g in range(GROUP)
    ]
    for h in range(GROUP // 4):
        slot = me ^ (step * (GROUP // 4) + h)
        for t in range(4):
            halves[slot & 1, slot >> 1, t] = products[4 * h + t]

    @pl.when(step == 0)
    def _():
        for h in range(4):
            slot = me ^ h
            for t in range(4):
                halves[slot & 1, slot >> 1, t] += spilled[4 * h + t].astype(F32)


def forward_split(ids, band, rows, rim, base, spilled, same, other, extended, halves):
    forward_kernel(ids, band, rows, rim, base, spilled, halves, extended)

    @pl.when(pl.program_id(0) == pl.num_programs(0) - 1)
    def _():
        same[...] = halves[0]
        other[...] = halves[1]


def band_forward(ids, band, rows, rim, base, spilled):
    return pl.pallas_call(
        forward_split,
        grid_spec=pltpu.PrefetchScalarGridSpec(
            num_scalar_prefetch=1,
            grid=(64 // GROUP,),
            in_specs=[
                pl.BlockSpec((GROUP, 256, 256), lambda i, *_: (i, 0, 0)),
                whole((64, 32, 256)),
                whole((16, 32, 256)),
                whole((64, 32, 256)),
                whole((16, 32, 256)),
            ],
            out_specs=[whole((8, 4, 32, 256))] * 2,
            scratch_shapes=[
                pltpu.VMEM((80, 32, 256), BF16),
                pltpu.VMEM((2, 8, 4, 32, 256), F32),
            ],
        ),
        out_shape=[jax.ShapeDtypeStruct((8, 4, 32, 256), F32)] * 2,
        compiler_params=params(),
        cost_estimate=pl.CostEstimate(
            flops=2 * 64 * 256 * 256 * 32, bytes_accessed=14 << 20, transcendentals=0
        ),
    )(ids, band, rows, rim, base, spilled)


def fold_kernel(same, arrived, *outs):
    for k in range(4):
        total = same[2 * k : 2 * k + 2] + arrived[2 * k : 2 * k + 2]
        outs[k][...] = total.astype(outs[k].dtype)


def fold(same, arrived):
    return pl.pallas_call(
        fold_kernel,
        out_shape=pair_shapes(),
        compiler_params=params(),
        cost_estimate=pl.CostEstimate(flops=0, bytes_accessed=3 << 20, transcendentals=0),
    )(same, arrived)


def against(left, right):
    return lax.dot_general(
        left, right, (((1,), (1,)), ((), ())), precision=PRECISE, preferred_element_type=F32
    )


def gram_kernel(n, with_images, *refs):
    basis, images = refs[: n + 1], refs[n + 1 : 2 * n + 1]
    terms = refs[2 * n + 1 : 2 * n + 5]
    mask, image_out, gram_out = refs[2 * n + 5 :]
    plain = jnp.zeros((32, 32 * (n + 1)), F32)
    cross = jnp.zeros((32, 32 * (n + 1)), F32)
    for t in range(4):
        image = ((terms[0][t] + terms[1][t]) + (terms[2][t] + terms[3][t])) * mask[t]
        image_out[t] = image
        newest = basis[-1][t]
        columns = jnp.concatenate([b[t] for b in basis], axis=0)
        plain += against(newest, columns)
        seen = jnp.concatenate([b[t] for b in images] + [image], axis=0)
        cross += 0.5 * (against(newest, seen) + against(image, columns))
    gram_out[...] = jnp.concatenate([plain, cross], axis=1)


def grams(older, older_images, newest, terms, mask):
    n = len(older)
    return pl.pallas_call(
        functools.partial(gram_kernel, n, True),
        out_shape=[
            jax.ShapeDtypeStruct((4, 32, 256), F32),
            jax.ShapeDtypeStruct((32, 64 * (n + 1)), F32),
        ],
        compiler_params=params(),
        cost_estimate=pl.CostEstimate(flops=1 << 27, bytes_accessed=1 << 20, transcendentals=0),
    )(*older, newest, *older_images, *terms, mask)


def mul(left, right):
    return jnp.dot(left, right, precision=PRECISE, preferred_element_type=F32)


def mul_left(left, right):
    return lax.dot_general(
        left, right, (((0,), (0,)), ((), ())), precision=PRECISE, preferred_element_type=F32
    )


def symmetric(matrix):
    return 0.5 * (matrix + matrix.T)


def unit(order):
    return (
        lax.broadcasted_iota(jnp.int32, (order, order), 0)
        == lax.broadcasted_iota(jnp.int32, (order, order), 1)
    ).astype(F32)


def block_inverse(matrix):
    order = matrix.shape[0]
    table = jnp.concatenate([matrix, unit(order)], axis=1)
    places = lax.broadcasted_iota(jnp.int32, (order, 1), 0)
    for k in range(order - 1):
        pivot = table[k : k + 1] / table[k : k + 1, k : k + 1]
        table = table - jnp.where(places > k, table[:, k : k + 1], 0.0) * pivot
    pivots = jnp.sum(table[:, :order] * unit(order), axis=1, keepdims=True)
    return table[:, order:] * lax.rsqrt(pivots)


def factor_inverse(matrix):
    order = matrix.shape[0]
    if order == 32:
        return block_inverse(matrix)
    head = block_inverse(matrix[:32, :32])
    edge = mul(head, matrix[:32, 32:])
    rest = factor_inverse(matrix[32:, 32:] - mul_left(edge, edge))
    lower = -mul(rest, mul_left(edge, head))
    return jnp.concatenate(
        [
            jnp.concatenate([head, jnp.zeros((32, order - 32), F32)], axis=1),
            jnp.concatenate([lower, rest], axis=1),
        ],
        axis=0,
    )


def joined(top, edge, corner):
    return jnp.concatenate(
        [jnp.concatenate([top, edge.T], axis=1), jnp.concatenate([edge, corner], axis=1)], axis=0
    )


def small_start(gram):
    inverse = block_inverse(symmetric(gram[:, :32]))
    return inverse, symmetric(against(mul(inverse, symmetric(gram[:, 32:])), inverse))


def small_step(known, known_images, gram):
    order = gram.shape[1] // 2
    edge = order - 32
    basis_gram = joined(known, gram[:, :edge], symmetric(gram[:, edge:order]))
    image_gram = joined(known_images, gram[:, order : order + edge], symmetric(gram[:, order + edge :]))
    head = lax.broadcasted_iota(jnp.int32, (1, order), 1) < 32
    down = lax.broadcasted_iota(jnp.int32, (order, 1), 0) < 32
    diagonal = basis_gram * unit(order)
    scale = jnp.where(head, 1.0, lax.rsqrt(jnp.sum(diagonal, axis=0, keepdims=True) + EPSILON))
    scale_down = jnp.where(down, 1.0, lax.rsqrt(jnp.sum(diagonal, axis=1, keepdims=True) + EPSILON))
    basis_gram = scale_down * basis_gram * scale
    image_gram = scale_down * image_gram * scale
    cross = basis_gram[32:, :32]
    tail = factor_inverse(basis_gram[32:, 32:] - against(cross, cross))
    inverse = jnp.concatenate(
        [
            jnp.concatenate([unit(32), jnp.zeros((32, edge), F32)], axis=1),
            jnp.concatenate([-mul(tail, cross), tail], axis=1),
        ],
        axis=0,
    )
    reduced = symmetric(against(mul(inverse, image_gram), inverse))
    size = jnp.sqrt(jnp.sum(jnp.sum(reduced * reduced, axis=1, keepdims=True), axis=0, keepdims=True))
    filtered = (reduced + size * unit(order)) / (2.0 * size)
    filtered = mul(filtered, filtered)
    leading = mul(filtered, filtered[:, :32])
    turned = mul(block_inverse(mul_left(leading, leading)), leading.T)
    weights = mul(turned, inverse)
    weights = jnp.concatenate([weights, jnp.where(head, 0.0, weights)], axis=0)
    next_basis = symmetric(against(mul(weights, basis_gram), weights))
    next_images = symmetric(against(mul(weights, image_gram), weights))
    return weights * scale, next_basis, next_images


def step_kernel(n, last, *refs):
    basis, images, mask, gram = refs[:n], refs[n : 2 * n], refs[2 * n], refs[2 * n + 1]
    if n == 1:
        outs = refs[2 * n + 2 :]
        weights, ritz = small_start(gram[...])
        next_basis, next_images = unit(32), ritz
    else:
        outs = refs[2 * n + 4 :]
        weights, next_basis, next_images = small_step(
            refs[2 * n + 2][...], refs[2 * n + 3][...], gram[...]
        )
        ritz = next_images[:32, :32]
    if last:
        outs[0][...] = ritz
        for t in range(4):
            outs[1][t] = mul(weights[:32], jnp.concatenate([b[t] for b in basis], axis=0))
        return
    outs[0][...] = next_basis
    outs[1][...] = next_images
    for t in range(4):
        moved = mul(weights, jnp.concatenate([b[t] for b in basis], axis=0))
        moved_images = mul(weights, jnp.concatenate([b[t] for b in images], axis=0))
        residual = moved_images[:32] - mul(ritz, moved[:32])
        outs[2][t] = (residual * mask[t]).astype(BF16)
        outs[3][t] = residual
        outs[4][t] = moved[:32]
        outs[5][t] = moved_images[:32]
        if n > 1:
            outs[6][t] = moved[32:]
            outs[7][t] = moved_images[32:]


def advance(basis, images, mask, gram, known, last=False):
    n = len(basis)
    slab = jax.ShapeDtypeStruct((4, 32, 256), F32)
    if last:
        outs = [jax.ShapeDtypeStruct((32, 32), F32), slab]
    else:
        order = 32 if n == 1 else 64
        outs = [jax.ShapeDtypeStruct((order, order), F32)] * 2
        outs += [jax.ShapeDtypeStruct((4, 32, 256), BF16)] + [slab] * (3 if n == 1 else 5)
    return pl.pallas_call(
        functools.partial(step_kernel, n, last),
        out_shape=outs,
        compiler_params=params(),
        cost_estimate=pl.CostEstimate(flops=1 << 28, bytes_accessed=1 << 20, transcendentals=0),
    )(*basis, *images, mask, gram, *known)


def body(x_start, bin_mask, band, off_tiles, off_rows, off_cols, off_count):
    width = x_start.shape[1]
    band = band[:, 0]
    tiles = off_tiles[0, 0]
    row_ids, col_ids = off_rows[0, 0], off_cols[0, 0]
    ids = jnp.stack(
        [lax.axis_index("brow"), lax.axis_index("bcol"), off_count[0, 0], jnp.int32(0)]
    ).astype(jnp.int32)
    mask = bin_mask.astype(F32).reshape(4, 1, 256)
    started = x_start.T.reshape(width, 4, 256).transpose(1, 0, 2) * mask

    def apply_operator(packed):
        pair = jnp.stack([packed, flip(packed, "bcol", 2)])
        near = [pair] + [flip(pair, "bcol", 4 * k) for k in (1, 2, 3)]
        across = [flip(part, "bcol", 1) for part in near]
        col_pair = jnp.stack([packed, flip(packed, "brow", 4)])
        along = [col_pair] + [flip(col_pair, "brow", k) for k in (1, 2, 3)]
        rows, rim, cols = assemble(ids, near + across + along)
        rim = shifted(rim, "brow", -1)
        spread, spill = band_back(ids, band, rows)
        spilled = shifted(spill, "brow", 1)
        base, *col_sums = far(ids, row_ids, col_ids, tiles, rows, cols, spread)
        c0, c1, c2, c3 = [col_sums[0]] + [
            flip(col_sums[k], "brow", k).astype(F32) for k in (1, 2, 3)
        ]
        col_total = (c0 + c1) + (c2 + c3)
        col_other = flip(col_total[1], "brow", 4)
        same, other = band_forward(ids, band, rows, rim, base, spilled)
        folded = fold(same, flip(other, "bcol", 1))
        r0, r1, r2, r3 = [folded[0]] + [
            flip(folded[k], "bcol", 4 * k).astype(F32) for k in (1, 2, 3)
        ]
        row_total = (r0 + r1) + (r2 + r3)
        row_other = flip(row_total[1], "bcol", 2)
        return [row_total[0], row_other, col_total[0], col_other]

    terms = apply_operator((started * mask).astype(BF16))
    image, gram = grams([], [], started, terms, mask)
    known_basis, known_images, packed, residual, vectors, images = advance(
        [started], [image], mask, sum_all(gram), []
    )
    older, older_images = [vectors], [images]
    for step in range(STEPS):
        terms = apply_operator(packed)
        residual_image, gram = grams(older, older_images, residual, terms, mask)
        outs = advance(
            older + [residual],
            older_images + [residual_image],
            mask,
            sum_all(gram),
            [known_basis, known_images],
            last=step == STEPS - 1,
        )
        if step < STEPS - 1:
            known_basis, known_images, packed, residual, vectors, images, tail, tail_images = outs
            older, older_images = [vectors, tail], [images, tail_images]
    ritz, vectors = outs
    return vectors.transpose(1, 0, 2).reshape(width, -1).T, ritz


def solution(mesh):
    return jax.shard_map(
        body,
        mesh=mesh,
        in_specs=(
            P(("brow", "bcol"), None),
            P(("brow", "bcol")),
            P("brow", "bcol", None, None),
            P("brow", "bcol", None, None, None),
            P("brow", "bcol", None),
            P("brow", "bcol", None),
            P("brow", "bcol"),
        ),
        out_specs=(P(("brow", "bcol"), None), P()),
        check_vma=False,
    )
```

```python
import functools

import jax
import jax.numpy as jnp
from jax import lax
from jax.experimental import pallas as pl
from jax.experimental.pallas import tpu as pltpu
from jax.sharding import PartitionSpec as P

STEPS = 3
PRECISE = lax.Precision.HIGHEST
EPSILON = 1e-06
F32 = jnp.float32
BF16 = jnp.bfloat16
GROUP = 16
VMEM_BYTES = 40 * 1024 * 1024
PAIR = (2, 4, 32, 256)


def flip(value, axis, by):
    length = lax.axis_size(axis)
    return lax.ppermute(value, axis, [(i, i ^ by) for i in range(length)])


def flip_both(value, row_by, col_by):
    rows, cols = lax.axis_size("brow"), lax.axis_size("bcol")
    pairs = [
        (r * cols + c, (r ^ row_by) * cols + (c ^ col_by)) for r in range(rows) for c in range(cols)
    ]
    return lax.ppermute(value, ("brow", "bcol"), pairs)


def shifted(value, axis, by):
    length = lax.axis_size(axis)
    pairs = [(i, i + by) for i in range(length) if 0 <= i + by < length]
    return lax.ppermute(value, axis, pairs)


def sum_all(value):
    value = value + flip(value, "bcol", 1)
    value = (value + flip(value, "bcol", 4)) + (flip(value, "bcol", 8) + flip(value, "bcol", 12))
    value = (value + flip(value, "brow", 1)) + (flip(value, "brow", 2) + flip(value, "brow", 3))
    value = (value + flip(value, "bcol", 2)) + (flip(value, "brow", 4) + flip_both(value, 4, 2))
    return value


def whole(shape):
    return pl.BlockSpec(shape, lambda *_: (0,) * len(shape))


def params():
    return pltpu.CompilerParams(vmem_limit_bytes=VMEM_BYTES)


def assemble_kernel(ids, p0, p1, p2, p3, q0, q1, q2, q3, c0, c1, c2, c3, rows_out, rim_out, cols_out):
    mine, me = ids[0], ids[1]
    near, across, along = (p0, p1, p2, p3), (q0, q1, q2, q3), (c0, c1, c2, c3)
    for k in range(4):
        for half in range(2):
            for parity, refs in ((0, near), (1, across)):
                slab = me ^ (4 * k + 2 * half + parity)
                rows_out[pl.ds(4 * slab, 4)] = refs[k][half]
            slab = mine ^ (4 * half + k)
            cols_out[pl.ds(4 * slab, 4)] = along[k][half]
    rim_out[...] = rows_out[:16]


def assemble(ids, parts):
    return pl.pallas_call(
        assemble_kernel,
        grid_spec=pltpu.PrefetchScalarGridSpec(
            num_scalar_prefetch=1,
            grid=(1,),
            in_specs=[whole((2, 4, 32, 256))] * 12,
            out_specs=[whole((64, 32, 256)), whole((16, 32, 256)), whole((32, 32, 256))],
        ),
        out_shape=[
            jax.ShapeDtypeStruct((64, 32, 256), BF16),
            jax.ShapeDtypeStruct((16, 32, 256), BF16),
            jax.ShapeDtypeStruct((32, 32, 256), BF16),
        ],
        compiler_params=params(),
        cost_estimate=pl.CostEstimate(flops=0, bytes_accessed=3 << 20, transcendentals=0),
    )(ids, *parts)


def back_kernel(ids, band, rows, spread, spill):
    me = ids[1]
    step = pl.program_id(0)

    @pl.when(step == 0)
    def _():
        spread[:16] = jnp.zeros((16, 32, 256), F32)
        spread[64:] = jnp.zeros((16, 32, 256), F32)

    first = step * GROUP
    products = [
        jnp.dot(rows[first + g], band[g], preferred_element_type=F32) for g in range(GROUP)
    ]
    for g in range(GROUP):
        spread[first + g + me] = products[g]

    @pl.when(step == pl.num_programs(0) - 1)
    def _():
        for half in range(2):
            for parity in range(2):
                slab = (me & 3) ^ (2 * half + parity)
                spill[parity, half] = spread[pl.ds(64 + 4 * slab, 4)].astype(BF16)


def band_back(ids, band, rows):
    return pl.pallas_call(
        back_kernel,
        grid_spec=pltpu.PrefetchScalarGridSpec(
            num_scalar_prefetch=1,
            grid=(64 // GROUP,),
            in_specs=[
                pl.BlockSpec((GROUP, 256, 256), lambda i, *_: (i, 0, 0)),
                whole((64, 32, 256)),
            ],
            out_specs=[whole((80, 32, 256)), whole((2,) + PAIR)],
        ),
        out_shape=[
            jax.ShapeDtypeStruct((80, 32, 256), F32),
            jax.ShapeDtypeStruct((2,) + PAIR, BF16),
        ],
        compiler_params=params(),
        cost_estimate=pl.CostEstimate(
            flops=2 * 64 * 256 * 256 * 32, bytes_accessed=11 << 20, transcendentals=0
        ),
    )(ids, band, rows)


def far_kernel(ids, row_ids, col_ids, tiles, rows, cols, base, out, acc, k0, k1, k2, k3):
    mine, count = ids[0], ids[2]
    step = pl.program_id(0)

    @pl.when(step == 0)
    def _():
        out[...] = base[...]
        acc[...] = jnp.zeros_like(acc)

    def visit(base_slot, partial):
        first = step * GROUP + base_slot
        found = []
        for g in range(8):
            i = first + g
            live = i < count
            a, b = row_ids[i], col_ids[i]
            if partial:
                a, b = jnp.where(live, a, 0), jnp.where(live, b, 0)
            tile = tiles[base_slot + g]
            forward = lax.dot_general(
                cols[b], tile, (((1,), (1,)), ((), ())), preferred_element_type=F32
            )
            back = jnp.dot(rows[a], tile, preferred_element_type=F32)
            if partial:
                forward, back = jnp.where(live, forward, 0.0), jnp.where(live, back, 0.0)
            found.append((a, b, forward, back))
        for a, b, forward, back in found:
            out[a] += forward
            acc[b] += back

    for h in range(0, GROUP, 8):
        first = step * GROUP + h

        @pl.when(first + 8 <= count)
        def _():
            visit(h, False)

        @pl.when((first + 8 > count) & (first < count))
        def _():
            visit(h, True)

    @pl.when(step == pl.num_programs(0) - 1)
    def _():
        for j in range(8):
            piece = acc[pl.ds(4 * (mine ^ j), 4)]
            target = (k0, k1, k2, k3)[j & 3]
            target[j >> 2] = piece.astype(target.dtype)


def pair_shapes():
    return [jax.ShapeDtypeStruct(PAIR, F32)] + [jax.ShapeDtypeStruct(PAIR, BF16)] * 3


def far(ids, row_ids, col_ids, tiles, rows, cols, base):
    return pl.pallas_call(
        far_kernel,
        grid_spec=pltpu.PrefetchScalarGridSpec(
            num_scalar_prefetch=3,
            grid=(64 // GROUP,),
            in_specs=[
                pl.BlockSpec((GROUP, 256, 256), lambda i, *_: (i, 0, 0)),
                whole((64, 32, 256)),
                whole((32, 32, 256)),
                whole((64, 32, 256)),
            ],
            out_specs=[whole((64, 32, 256)), whole((32, 32, 256))] + [whole(PAIR)] * 4,
        ),
        out_shape=[
            jax.ShapeDtypeStruct((64, 32, 256), F32),
            jax.ShapeDtypeStruct((32, 32, 256), F32),
        ]
        + pair_shapes(),
        compiler_params=params(),
        cost_estimate=pl.CostEstimate(
            flops=4 * 64 * 256 * 256 * 32, bytes_accessed=15 << 20, transcendentals=0
        ),
    )(ids, row_ids, col_ids, tiles, rows, cols, base)


def forward_kernel(ids, band, rows, rim, base, same, other, extended, halves):
    me = ids[1]
    step = pl.program_id(0)

    @pl.when(step == 0)
    def _():
        extended[:64] = rows[...]
        extended[64:80] = rim[...]

    first = step * GROUP
    products = [
        lax.dot_general(
            extended[first + g + me], band[g], (((1,), (1,)), ((), ())), preferred_element_type=F32
        )
        + base[first + g]
        for g in range(GROUP)
    ]
    for h in range(GROUP // 4):
        slot = me ^ (step * (GROUP // 4) + h)
        for t in range(4):
            halves[slot & 1, slot >> 1, t] = products[4 * h + t]

    @pl.when(step == pl.num_programs(0) - 1)
    def _():
        same[...] = halves[0]
        other[...] = halves[1]


def band_forward(ids, band, rows, rim, base):
    return pl.pallas_call(
        forward_kernel,
        grid_spec=pltpu.PrefetchScalarGridSpec(
            num_scalar_prefetch=1,
            grid=(64 // GROUP,),
            in_specs=[
                pl.BlockSpec((GROUP, 256, 256), lambda i, *_: (i, 0, 0)),
                whole((64, 32, 256)),
                whole((16, 32, 256)),
                whole((64, 32, 256)),
            ],
            out_specs=[whole((8, 4, 32, 256))] * 2,
            scratch_shapes=[
                pltpu.VMEM((80, 32, 256), BF16),
                pltpu.VMEM((2, 8, 4, 32, 256), F32),
            ],
        ),
        out_shape=[jax.ShapeDtypeStruct((8, 4, 32, 256), F32)] * 2,
        compiler_params=params(),
        cost_estimate=pl.CostEstimate(
            flops=0, bytes_accessed=1 << 16, transcendentals=0
        ),
    )(ids, band, rows, rim, base)


def fold_kernel(ids, same, arrived, spilled, spilled_across, *outs):
    here = ids[1] >> 2
    extra = spilled[0].astype(F32) + spilled_across[...].astype(F32)
    for k in range(4):
        total = same[2 * k : 2 * k + 2] + arrived[2 * k : 2 * k + 2]
        total = total + jnp.where(here == k, extra, 0.0)
        outs[k][...] = total.astype(outs[k].dtype)


def fold(ids, same, arrived, spilled, spilled_across):
    return pl.pallas_call(
        fold_kernel,
        grid_spec=pltpu.PrefetchScalarGridSpec(
            num_scalar_prefetch=1,
            grid=(1,),
            in_specs=[whole((8, 4, 32, 256)), whole((8, 4, 32, 256)), whole((2,) + PAIR), whole(PAIR)],
            out_specs=[whole(PAIR)] * 4,
        ),
        out_shape=pair_shapes(),
        compiler_params=params(),
        cost_estimate=pl.CostEstimate(flops=0, bytes_accessed=3 << 20, transcendentals=0),
    )(ids, same, arrived, spilled, spilled_across)


def against(left, right):
    return lax.dot_general(
        left, right, (((1,), (1,)), ((), ())), precision=PRECISE, preferred_element_type=F32
    )


def image_gram_kernel(n, ids, same, other, cols, spread, *refs):
    evens, odds, alongs, rims, out = refs[:n], refs[n : 2 * n], refs[2 * n : 3 * n], refs[3 * n : 4 * n], refs[-1]

    @pl.when(pl.program_id(0) == 0)
    def _():
        out[...] = jnp.zeros_like(out)

    total = jnp.zeros((32, 32 * n), F32)
    jobs = [(same.at[0], [r.at[0] for r in evens], 4), (other.at[0], [r.at[0] for r in odds], 4)]
    jobs += [(cols, alongs, 4), (spread, rims, 2)]
    for part, known, count in jobs:
        for t in range(count):
            columns = jnp.concatenate([k[t] for k in known], axis=0)
            total += lax.dot_general(
                part[t].astype(BF16), columns, (((1,), (1,)), ((), ())), preferred_element_type=F32
            )
    out[...] += total


def image_grams(ids, same, other, cols, spread, gathered):
    n = len(gathered)
    slab = (1, 4, 32, 256)
    at_even = pl.BlockSpec(slab, lambda e, ids: (ids[1] ^ (2 * e), 0, 0, 0))
    at_odd = pl.BlockSpec(slab, lambda e, ids: (ids[1] ^ (2 * e + 1), 0, 0, 0))
    at_slab = pl.BlockSpec(slab, lambda e, ids: (e, 0, 0, 0))
    four = pl.BlockSpec((4, 32, 256), lambda e, ids: (e, 0, 0))
    two = pl.BlockSpec((2, 32, 256), lambda e, ids: (e, 0, 0))
    over = pl.BlockSpec((2, 32, 256), lambda e, ids: (32 + e, 0, 0))
    rows = [g[0].reshape(16, 4, 32, 256) for g in gathered]
    return pl.pallas_call(
        functools.partial(image_gram_kernel, n),
        grid_spec=pltpu.PrefetchScalarGridSpec(
            num_scalar_prefetch=1,
            grid=(8,),
            in_specs=[at_slab, at_slab, four, over]
            + [at_even] * n
            + [at_odd] * n
            + [four] * n
            + [two] * n,
            out_specs=whole((32, 32 * n)),
        ),
        out_shape=jax.ShapeDtypeStruct((32, 32 * n), F32),
        compiler_params=params(),
        cost_estimate=pl.CostEstimate(flops=1 << 28, bytes_accessed=8 << 20, transcendentals=0),
    )(ids, same, other, cols, spread, *rows, *rows, *[g[1] for g in gathered], *[g[2] for g in gathered])


def gram_kernel(n, *refs):
    basis, images, out = refs[: n + 1], refs[n + 1 : 2 * n + 1], refs[-1]
    total = jnp.zeros((32, 32 * (2 * n + 1)), F32)
    for t in range(4):
        columns = jnp.concatenate([b[t] for b in basis] + [b[t] for b in images], axis=0)
        total += against(basis[-1][t], columns)
    out[...] = total


def grams(older, older_images, newest):
    n = len(older)
    return pl.pallas_call(
        functools.partial(gram_kernel, n),
        out_shape=jax.ShapeDtypeStruct((32, 32 * (2 * n + 1)), F32),
        compiler_params=params(),
        cost_estimate=pl.CostEstimate(flops=1 << 27, bytes_accessed=1 << 20, transcendentals=0),
    )(*older, newest, *older_images)


def mul(left, right):
    return jnp.dot(left, right, precision=PRECISE, preferred_element_type=F32)


def mul_left(left, right):
    return lax.dot_general(
        left, right, (((0,), (0,)), ((), ())), precision=PRECISE, preferred_element_type=F32
    )


def symmetric(matrix):
    return 0.5 * (matrix + matrix.T)


def unit(order):
    return (
        lax.broadcasted_iota(jnp.int32, (order, order), 0)
        == lax.broadcasted_iota(jnp.int32, (order, order), 1)
    ).astype(F32)


def block_inverse(matrix):
    order = matrix.shape[0]
    table = jnp.concatenate([matrix, unit(order)], axis=1)
    places = lax.broadcasted_iota(jnp.int32, (order, 2 * order), 0)
    for k in range(0, order, 2):
        left = jnp.broadcast_to(table[:, k : k + 1], table.shape)
        right = jnp.broadcast_to(table[:, k + 1 : k + 2], table.shape)
        share = right[k : k + 1] / left[k : k + 1]
        top = table[k : k + 1] / left[k : k + 1]
        corner = right[k + 1 : k + 2] - share * right[k : k + 1]
        second = (table[k + 1 : k + 2] - share * table[k : k + 1]) / corner
        table = (
            table
            - jnp.where(places > k, left, 0.0) * top
            - jnp.where(places > k + 1, right - left * share, 0.0) * second
        )
    pivots = jnp.sum(table[:, :order] * unit(order), axis=1, keepdims=True)
    return table[:, order:] * lax.rsqrt(pivots)


def factor_inverse(matrix):
    order = matrix.shape[0]
    if order == 32:
        return block_inverse(matrix)
    head = block_inverse(matrix[:32, :32])
    edge = mul(head, matrix[:32, 32:])
    rest = factor_inverse(matrix[32:, 32:] - mul_left(edge, edge))
    lower = -mul(rest, mul_left(edge, head))
    return jnp.concatenate(
        [
            jnp.concatenate([head, jnp.zeros((32, order - 32), F32)], axis=1),
            jnp.concatenate([lower, rest], axis=1),
        ],
        axis=0,
    )


def joined(top, edge, corner):
    return jnp.concatenate(
        [jnp.concatenate([top, edge.T], axis=1), jnp.concatenate([edge, corner], axis=1)], axis=0
    )


def small_start(gram):
    inverse = block_inverse(symmetric(gram[:, :32]))
    return inverse, symmetric(against(mul(inverse, symmetric(gram[:, 32:])), inverse))


def small_step(known, known_images, origin, gram, image_part):
    edge = known.shape[0]
    order = edge + 32
    seen = origin.shape[1]
    basis_gram = joined(known, gram[:, :edge], symmetric(gram[:, edge:order]))
    cross_images = 0.5 * (gram[:, order:] + against(image_part[:, :seen], origin))
    image_gram = joined(known_images, cross_images, symmetric(image_part[:, seen:]))
    head = lax.broadcasted_iota(jnp.int32, (1, order), 1) < 32
    down = lax.broadcasted_iota(jnp.int32, (order, 1), 0) < 32
    diagonal = basis_gram * unit(order)
    scale = jnp.where(head, 1.0, lax.rsqrt(jnp.sum(diagonal, axis=0, keepdims=True) + EPSILON))
    scale_down = jnp.where(down, 1.0, lax.rsqrt(jnp.sum(diagonal, axis=1, keepdims=True) + EPSILON))
    basis_gram = scale_down * basis_gram * scale
    image_gram = scale_down * image_gram * scale
    cross = basis_gram[32:, :32]
    tail = factor_inverse(basis_gram[32:, 32:] - against(cross, cross))
    inverse = jnp.concatenate(
        [
            jnp.concatenate([unit(32), jnp.zeros((32, edge), F32)], axis=1),
            jnp.concatenate([-mul(tail, cross), tail], axis=1),
        ],
        axis=0,
    )
    reduced = symmetric(against(mul(inverse, image_gram), inverse))
    size = jnp.sqrt(jnp.sum(jnp.sum(reduced * reduced, axis=1, keepdims=True), axis=0, keepdims=True))
    filtered = (reduced + size * unit(order)) / (2.0 * size)
    filtered = mul(filtered, filtered)
    leading = mul(filtered, filtered[:, :32])
    turned = mul(block_inverse(mul_left(leading, leading)), leading.T)
    weights = mul(turned, inverse)
    weights = jnp.concatenate([weights, jnp.where(head, 0.0, weights)], axis=0)
    next_basis = symmetric(against(mul(weights, basis_gram), weights))
    next_images = symmetric(against(mul(weights, image_gram), weights))
    weights = weights * scale
    next_origin = jnp.concatenate([mul(weights[:, :edge], origin), weights[:, edge:]], axis=1)
    return weights, next_basis, next_images, next_origin


def algebra_kernel(first, *refs):
    if first:
        gram, weights_out, ritz_out = refs
        weights_out[...], ritz_out[...] = small_start(gram[...])
        return
    width = 2 * refs[0].shape[0] + 32
    known, known_images, origin, gram = (r[...] for r in refs[:4])
    results = small_step(known, known_images, origin, gram[:, :width], gram[:, width:])
    for out, value in zip(refs[4:], results):
        out[...] = value


def algebra(gram, known):
    if not known:
        shapes = [(32, 32), (32, 32)]
    else:
        shapes = [(64, known[0].shape[0] + 32), (64, 64), (64, 64), (64, known[2].shape[1] + 32)]
    return pl.pallas_call(
        functools.partial(algebra_kernel, not known),
        out_shape=[jax.ShapeDtypeStruct(s, F32) for s in shapes],
        compiler_params=params(),
        cost_estimate=pl.CostEstimate(flops=1 << 28, bytes_accessed=20 << 20, transcendentals=0),
    )(*known, gram)


def update_kernel(n, *refs):
    basis, images, terms = refs[:n], refs[n : 2 * n - 1], refs[2 * n - 1 : 2 * n + 3]
    mask, weights, ritz = refs[2 * n + 3], refs[2 * n + 4][...], refs[2 * n + 5][:32, :32]
    outs = refs[2 * n + 6 :]
    for t in range(4):
        newest = ((terms[0][t] + terms[1][t]) + (terms[2][t] + terms[3][t])) * mask[t]
        moved = mul(weights, jnp.concatenate([b[t] for b in basis], axis=0))
        moved_images = mul(weights, jnp.concatenate([b[t] for b in images] + [newest], axis=0))
        residual = moved_images[:32] - mul(ritz, moved[:32])
        outs[0][t] = (residual * mask[t]).astype(BF16)
        outs[1][t] = residual
        outs[2][t] = moved[:32]
        outs[3][t] = moved_images[:32]
        if n > 1:
            outs[4][t] = moved[32:]
            outs[5][t] = moved_images[32:]


def update(basis, images, terms, mask, weights, ritz):
    n = len(basis)
    slab = jax.ShapeDtypeStruct((4, 32, 256), F32)
    return pl.pallas_call(
        functools.partial(update_kernel, n),
        out_shape=[jax.ShapeDtypeStruct((4, 32, 256), BF16)] + [slab] * (3 if n == 1 else 5),
        compiler_params=params(),
        cost_estimate=pl.CostEstimate(flops=1 << 27, bytes_accessed=1 << 20, transcendentals=0),
    )(*basis, *images, *terms, mask, weights, ritz)


def finish_kernel(n, *refs):
    basis, weights, out = refs[:n], refs[n][:32], refs[n + 1]
    for t in range(4):
        out[t] = mul(weights, jnp.concatenate([b[t] for b in basis], axis=0))


def finish(basis, weights):
    return pl.pallas_call(
        functools.partial(finish_kernel, len(basis)),
        out_shape=jax.ShapeDtypeStruct((4, 32, 256), F32),
        compiler_params=params(),
    )(*basis, weights)


def body(x_start, bin_mask, band, off_tiles, off_rows, off_cols, off_count):
    width = x_start.shape[1]
    band = band[:, 0]
    tiles = off_tiles[0, 0]
    row_ids, col_ids = off_rows[0, 0], off_cols[0, 0]
    ids = jnp.stack(
        [lax.axis_index("brow"), lax.axis_index("bcol"), off_count[0, 0], jnp.int32(0)]
    ).astype(jnp.int32)
    mask = bin_mask.astype(F32).reshape(4, 1, 256)
    started = x_start.T.reshape(width, 4, 256).transpose(1, 0, 2) * mask

    gathered = []

    def apply_operator(packed, plain, last=False):
        pair = jnp.stack([packed, flip(packed, "bcol", 2)])
        near = [pair] + [flip(pair, "bcol", 4 * k) for k in (1, 2, 3)]
        across = [flip(part, "bcol", 1) for part in near]
        col_pair = jnp.stack([packed, flip(packed, "brow", 4)])
        along = [col_pair] + [flip(col_pair, "brow", k) for k in (1, 2, 3)]
        rows, rim, cols = assemble(ids, near + across + along)
        rim = shifted(rim, "brow", -1)
        gathered.append((rows, cols, rim))
        spread, spill = band_back(ids, band, rows)
        if not last:
            spilled = shifted(spill, "brow", 1)
        base, col_all, *col_sums = far(ids, row_ids, col_ids, tiles, rows, cols, spread)
        same, other = band_forward(ids, band, rows, rim, base)
        image_part = image_grams(ids, same, other, col_all, spread, gathered)
        gram = sum_all(jnp.concatenate([plain, image_part], axis=1))
        if last:
            return gram, None
        other, spilled = lax.optimization_barrier((other, spilled))
        arrived = flip(other, "bcol", 1)
        folded = fold(ids, same, arrived, spilled, flip(spilled[1], "bcol", 1))
        folded, col_sums = lax.optimization_barrier((folded, col_sums))
        c0, c1, c2, c3 = [col_sums[0]] + [
            flip(col_sums[k], "brow", k).astype(F32) for k in (1, 2, 3)
        ]
        col_total = (c0 + c1) + (c2 + c3)
        col_other = flip(col_total[1], "brow", 4)
        r0, r1, r2, r3 = [folded[0]] + [
            flip(folded[k], "bcol", 4 * k).astype(F32) for k in (1, 2, 3)
        ]
        row_total = (r0 + r1) + (r2 + r3)
        row_other = flip(row_total[1], "bcol", 2)
        return gram, [row_total[0], row_other, col_total[0], col_other]

    gram, terms = apply_operator((started * mask).astype(BF16), grams([], [], started))
    weights, ritz = algebra(gram, [])
    known = [jnp.eye(width, dtype=F32), ritz, weights]
    packed, residual, vectors, images = update([started], [], terms, mask, weights, ritz)
    older, older_images = [vectors], [images]
    for step in range(STEPS):
        last = step == STEPS - 1
        gram, terms = apply_operator(packed, grams(older, older_images, residual), last)
        weights, *known = algebra(gram, known)
        basis = older + [residual]
        if not last:
            packed, residual, vectors, images, tail, tail_images = update(
                basis, older_images, terms, mask, weights, known[1]
            )
            older, older_images = [vectors, tail], [images, tail_images]
    vectors = finish(basis, weights)
    return vectors.transpose(1, 0, 2).reshape(width, -1).T, known[1][:width, :width]


def solution(mesh):
    return jax.shard_map(
        body,
        mesh=mesh,
        in_specs=(
            P(("brow", "bcol"), None),
            P(("brow", "bcol")),
            P("brow", "bcol", None, None),
            P("brow", "bcol", None, None, None),
            P("brow", "bcol", None),
            P("brow", "bcol", None),
            P("brow", "bcol"),
        ),
        out_specs=(P(("brow", "bcol"), None), P()),
        check_vma=False,
    )
```

```python
import functools

import jax
import jax.numpy as jnp
from jax import lax
from jax.experimental import pallas as pl
from jax.experimental.pallas import tpu as pltpu
from jax.sharding import PartitionSpec as P

STEPS = 3
PRECISE = lax.Precision.HIGHEST
EPSILON = 1e-06
F32 = jnp.float32
BF16 = jnp.bfloat16
GROUP = 16
VMEM_BYTES = 24 * 1024 * 1024
STREAM_BYTES = 58 * 1024 * 1024
PAIR = (2, 4, 32, 256)


def flip(value, axis, by):
    length = lax.axis_size(axis)
    return lax.ppermute(value, axis, [(i, i ^ by) for i in range(length)])


def flip_both(value, row_by, col_by):
    rows, cols = lax.axis_size("brow"), lax.axis_size("bcol")
    pairs = [
        (r * cols + c, (r ^ row_by) * cols + (c ^ col_by)) for r in range(rows) for c in range(cols)
    ]
    return lax.ppermute(value, ("brow", "bcol"), pairs)


def shifted(value, axis, by):
    length = lax.axis_size(axis)
    pairs = [(i, i + by) for i in range(length) if 0 <= i + by < length]
    return lax.ppermute(value, axis, pairs)


def sum_all(value):
    value = value + flip(value, "bcol", 1)
    value = (value + flip(value, "bcol", 4)) + (flip(value, "bcol", 8) + flip(value, "bcol", 12))
    value = (value + flip(value, "brow", 1)) + (flip(value, "brow", 2) + flip(value, "brow", 3))
    value = (value + flip(value, "bcol", 2)) + (flip(value, "brow", 4) + flip_both(value, 4, 2))
    return value


def whole(shape):
    return pl.BlockSpec(shape, lambda *_: (0,) * len(shape))


def params(limit=VMEM_BYTES):
    return pltpu.CompilerParams(vmem_limit_bytes=limit)


def assemble_kernel(ids, p0, p1, p2, p3, q0, q1, q2, q3, c0, c1, c2, c3, rows_out, rim_out, cols_out):
    mine, me = ids[0], ids[1]
    near, across, along = (p0, p1, p2, p3), (q0, q1, q2, q3), (c0, c1, c2, c3)
    for k in range(4):
        for half in range(2):
            for parity, refs in ((0, near), (1, across)):
                slab = me ^ (4 * k + 2 * half + parity)
                rows_out[pl.ds(4 * slab, 4)] = refs[k][half]
            slab = mine ^ (4 * half + k)
            cols_out[pl.ds(4 * slab, 4)] = along[k][half]
    rim_out[...] = rows_out[:16]


def assemble(ids, parts):
    return pl.pallas_call(
        assemble_kernel,
        grid_spec=pltpu.PrefetchScalarGridSpec(
            num_scalar_prefetch=1,
            grid=(1,),
            in_specs=[whole((2, 4, 32, 256))] * 12,
            out_specs=[whole((64, 32, 256)), whole((16, 32, 256)), whole((32, 32, 256))],
        ),
        out_shape=[
            jax.ShapeDtypeStruct((64, 32, 256), BF16),
            jax.ShapeDtypeStruct((16, 32, 256), BF16),
            jax.ShapeDtypeStruct((32, 32, 256), BF16),
        ],
        compiler_params=params(),
        cost_estimate=pl.CostEstimate(flops=0, bytes_accessed=3 << 20, transcendentals=0),
    )(ids, *parts)


def back_kernel(ids, band, rows, spread, spill):
    me = ids[1]
    step = pl.program_id(0)

    @pl.when(step == 0)
    def _():
        spread[:16] = jnp.zeros((16, 32, 256), F32)
        spread[64:] = jnp.zeros((16, 32, 256), F32)

    first = step * GROUP
    products = [
        jnp.dot(rows[first + g], band[g], preferred_element_type=F32) for g in range(GROUP)
    ]
    for g in range(GROUP):
        spread[first + g + me] = products[g]

    @pl.when(step == pl.num_programs(0) - 1)
    def _():
        for half in range(2):
            for parity in range(2):
                slab = (me & 3) ^ (2 * half + parity)
                spill[parity, half] = spread[pl.ds(64 + 4 * slab, 4)].astype(BF16)


def band_back(ids, band, rows, limit):
    return pl.pallas_call(
        back_kernel,
        grid_spec=pltpu.PrefetchScalarGridSpec(
            num_scalar_prefetch=1,
            grid=(64 // GROUP,),
            in_specs=[
                pl.BlockSpec((GROUP, 256, 256), lambda i, *_: (i, 0, 0)),
                whole((64, 32, 256)),
            ],
            out_specs=[whole((80, 32, 256)), whole((2,) + PAIR)],
        ),
        out_shape=[
            jax.ShapeDtypeStruct((80, 32, 256), F32),
            jax.ShapeDtypeStruct((2,) + PAIR, BF16),
        ],
        compiler_params=params(limit),
        cost_estimate=pl.CostEstimate(
            flops=2 * 64 * 256 * 256 * 32, bytes_accessed=11 << 20, transcendentals=0
        ),
    )(ids, band, rows)


def far_kernel(ids, row_ids, col_ids, tiles, rows, cols, out, acc, k0, k1, k2, k3):
    mine, count = ids[0], ids[2]
    step = pl.program_id(0)

    @pl.when(step == 0)
    def _():
        out[...] = jnp.zeros_like(out)
        acc[...] = jnp.zeros_like(acc)

    def visit(base_slot, partial):
        first = step * GROUP + base_slot
        found = []
        for g in range(8):
            i = first + g
            live = i < count
            a, b = row_ids[i], col_ids[i]
            if partial:
                a, b = jnp.where(live, a, 0), jnp.where(live, b, 0)
            tile = tiles[base_slot + g]
            forward = lax.dot_general(
                cols[b], tile, (((1,), (1,)), ((), ())), preferred_element_type=F32
            )
            back = jnp.dot(rows[a], tile, preferred_element_type=F32)
            if partial:
                forward, back = jnp.where(live, forward, 0.0), jnp.where(live, back, 0.0)
            found.append((a, b, forward, back))
        for a, b, forward, back in found:
            out[a] += forward
            acc[b] += back

    for h in range(0, GROUP, 8):
        first = step * GROUP + h

        @pl.when(first + 8 <= count)
        def _():
            visit(h, False)

        @pl.when((first + 8 > count) & (first < count))
        def _():
            visit(h, True)

    @pl.when(step == pl.num_programs(0) - 1)
    def _():
        for j in range(8):
            piece = acc[pl.ds(4 * (mine ^ j), 4)]
            target = (k0, k1, k2, k3)[j & 3]
            target[j >> 2] = piece.astype(target.dtype)


def pair_shapes():
    return [jax.ShapeDtypeStruct(PAIR, F32)] + [jax.ShapeDtypeStruct(PAIR, BF16)] * 3


def far(ids, row_ids, col_ids, tiles, rows, cols, limit):
    return pl.pallas_call(
        far_kernel,
        grid_spec=pltpu.PrefetchScalarGridSpec(
            num_scalar_prefetch=3,
            grid=(64 // GROUP,),
            in_specs=[
                pl.BlockSpec((GROUP, 256, 256), lambda i, *_: (i, 0, 0)),
                whole((64, 32, 256)),
                whole((32, 32, 256)),
            ],
            out_specs=[whole((64, 32, 256)), whole((32, 32, 256))] + [whole(PAIR)] * 4,
        ),
        out_shape=[
            jax.ShapeDtypeStruct((64, 32, 256), F32),
            jax.ShapeDtypeStruct((32, 32, 256), F32),
        ]
        + pair_shapes(),
        compiler_params=params(limit),
        cost_estimate=pl.CostEstimate(
            flops=4 * 64 * 256 * 256 * 32, bytes_accessed=15 << 20, transcendentals=0
        ),
    )(ids, row_ids, col_ids, tiles, rows, cols)


def forward_kernel(ids, band, rows, rim, spread, away, same, other, extended, halves):
    me = ids[1]
    step = pl.program_id(0)

    @pl.when(step == 0)
    def _():
        extended[:64] = rows[...]
        extended[64:80] = rim[...]

    first = step * GROUP
    products = [
        lax.dot_general(
            extended[first + g + me], band[g], (((1,), (1,)), ((), ())), preferred_element_type=F32
        )
        + (spread[g] + away[g])
        for g in range(GROUP)
    ]
    for h in range(GROUP // 4):
        slot = me ^ (step * (GROUP // 4) + h)
        for t in range(4):
            halves[slot & 1, slot >> 1, t] = products[4 * h + t]

    @pl.when(step == pl.num_programs(0) - 1)
    def _():
        same[...] = halves[0]
        other[...] = halves[1]


def band_forward(ids, band, rows, rim, spread, away):
    return pl.pallas_call(
        forward_kernel,
        grid_spec=pltpu.PrefetchScalarGridSpec(
            num_scalar_prefetch=1,
            grid=(64 // GROUP,),
            in_specs=[
                pl.BlockSpec((GROUP, 256, 256), lambda i, *_: (i, 0, 0)),
                whole((64, 32, 256)),
                whole((16, 32, 256)),
                pl.BlockSpec((GROUP, 32, 256), lambda i, *_: (i, 0, 0)),
                pl.BlockSpec((GROUP, 32, 256), lambda i, *_: (i, 0, 0)),
            ],
            out_specs=[whole((8, 4, 32, 256))] * 2,
            scratch_shapes=[
                pltpu.VMEM((80, 32, 256), BF16),
                pltpu.VMEM((2, 8, 4, 32, 256), F32),
            ],
        ),
        out_shape=[jax.ShapeDtypeStruct((8, 4, 32, 256), F32)] * 2,
        compiler_params=params(),
        cost_estimate=pl.CostEstimate(
            flops=0, bytes_accessed=1 << 16, transcendentals=0
        ),
    )(ids, band, rows, rim, spread, away)


def fold_kernel(ids, same, arrived, spilled, spilled_across, *outs):
    here = ids[1] >> 2
    extra = spilled[0].astype(F32) + spilled_across[...].astype(F32)
    for k in range(4):
        total = same[2 * k : 2 * k + 2] + arrived[2 * k : 2 * k + 2]
        total = total + jnp.where(here == k, extra, 0.0)
        outs[k][...] = total.astype(outs[k].dtype)


def fold(ids, same, arrived, spilled, spilled_across):
    return pl.pallas_call(
        fold_kernel,
        grid_spec=pltpu.PrefetchScalarGridSpec(
            num_scalar_prefetch=1,
            grid=(1,),
            in_specs=[whole((8, 4, 32, 256)), whole((8, 4, 32, 256)), whole((2,) + PAIR), whole(PAIR)],
            out_specs=[whole(PAIR)] * 4,
        ),
        out_shape=pair_shapes(),
        compiler_params=params(),
        cost_estimate=pl.CostEstimate(flops=0, bytes_accessed=3 << 20, transcendentals=0),
    )(ids, same, arrived, spilled, spilled_across)


def against(left, right):
    return lax.dot_general(
        left, right, (((1,), (1,)), ((), ())), precision=PRECISE, preferred_element_type=F32
    )


def image_gram_kernel(n, ids, same, other, cols, spread, *refs):
    evens, odds, alongs, rims, out = refs[:n], refs[n : 2 * n], refs[2 * n : 3 * n], refs[3 * n : 4 * n], refs[-1]

    @pl.when(pl.program_id(0) == 0)
    def _():
        out[...] = jnp.zeros_like(out)

    total = jnp.zeros((32, 32 * n), F32)
    jobs = [(same.at[0], [r.at[0] for r in evens], 4), (other.at[0], [r.at[0] for r in odds], 4)]
    jobs += [(cols, alongs, 4), (spread, rims, 2)]
    for part, known, count in jobs:
        for t in range(count):
            columns = jnp.concatenate([k[t] for k in known], axis=0)
            total += lax.dot_general(
                part[t].astype(BF16), columns, (((1,), (1,)), ((), ())), preferred_element_type=F32
            )
    out[...] += total


def image_grams(ids, same, other, cols, spread, gathered):
    n = len(gathered)
    slab = (1, 4, 32, 256)
    at_even = pl.BlockSpec(slab, lambda e, ids: (ids[1] ^ (2 * e), 0, 0, 0))
    at_odd = pl.BlockSpec(slab, lambda e, ids: (ids[1] ^ (2 * e + 1), 0, 0, 0))
    at_slab = pl.BlockSpec(slab, lambda e, ids: (e, 0, 0, 0))
    four = pl.BlockSpec((4, 32, 256), lambda e, ids: (e, 0, 0))
    two = pl.BlockSpec((2, 32, 256), lambda e, ids: (e, 0, 0))
    over = pl.BlockSpec((2, 32, 256), lambda e, ids: (32 + e, 0, 0))
    rows = [g[0].reshape(16, 4, 32, 256) for g in gathered]
    return pl.pallas_call(
        functools.partial(image_gram_kernel, n),
        grid_spec=pltpu.PrefetchScalarGridSpec(
            num_scalar_prefetch=1,
            grid=(8,),
            in_specs=[at_slab, at_slab, four, over]
            + [at_even] * n
            + [at_odd] * n
            + [four] * n
            + [two] * n,
            out_specs=whole((32, 32 * n)),
        ),
        out_shape=jax.ShapeDtypeStruct((32, 32 * n), F32),
        compiler_params=params(),
        cost_estimate=pl.CostEstimate(flops=1 << 28, bytes_accessed=8 << 20, transcendentals=0),
    )(ids, same, other, cols, spread, *rows, *rows, *[g[1] for g in gathered], *[g[2] for g in gathered])


def gram_kernel(n, *refs):
    basis, images, out = refs[: n + 1], refs[n + 1 : 2 * n + 1], refs[-1]
    total = jnp.zeros((32, 32 * (2 * n + 1)), F32)
    for t in range(4):
        columns = jnp.concatenate([b[t] for b in basis] + [b[t] for b in images], axis=0)
        total += against(basis[-1][t], columns)
    out[...] = total


def grams(older, older_images, newest):
    n = len(older)
    return pl.pallas_call(
        functools.partial(gram_kernel, n),
        out_shape=jax.ShapeDtypeStruct((32, 32 * (2 * n + 1)), F32),
        compiler_params=params(),
        cost_estimate=pl.CostEstimate(flops=1 << 27, bytes_accessed=1 << 20, transcendentals=0),
    )(*older, newest, *older_images)


def mul(left, right):
    return jnp.dot(left, right, precision=PRECISE, preferred_element_type=F32)


def mul_left(left, right):
    return lax.dot_general(
        left, right, (((0,), (0,)), ((), ())), precision=PRECISE, preferred_element_type=F32
    )


def symmetric(matrix):
    return 0.5 * (matrix + matrix.T)


def unit(order):
    return (
        lax.broadcasted_iota(jnp.int32, (order, order), 0)
        == lax.broadcasted_iota(jnp.int32, (order, order), 1)
    ).astype(F32)


def block_inverse(matrix):
    order = matrix.shape[0]
    table = jnp.concatenate([matrix, unit(order)], axis=1)
    places = lax.broadcasted_iota(jnp.int32, (order, 2 * order), 0)
    for k in range(0, order, 2):
        left = jnp.broadcast_to(table[:, k : k + 1], table.shape)
        right = jnp.broadcast_to(table[:, k + 1 : k + 2], table.shape)
        inverse = 1.0 / left[k : k + 1]
        share = right[k : k + 1] * inverse
        top = table[k : k + 1] * inverse
        corner = right[k + 1 : k + 2] - share * right[k : k + 1]
        second = (table[k + 1 : k + 2] - share * table[k : k + 1]) / corner
        table = (
            table
            - jnp.where(places > k, left, 0.0) * top
            - jnp.where(places > k + 1, right - left * share, 0.0) * second
        )
    pivots = jnp.sum(table[:, :order] * unit(order), axis=1, keepdims=True)
    return table[:, order:] * lax.rsqrt(pivots)


def factor_inverse(matrix):
    order = matrix.shape[0]
    if order == 32:
        return block_inverse(matrix)
    head = block_inverse(matrix[:32, :32])
    edge = mul(head, matrix[:32, 32:])
    rest = factor_inverse(matrix[32:, 32:] - mul_left(edge, edge))
    lower = -mul(rest, mul_left(edge, head))
    return jnp.concatenate(
        [
            jnp.concatenate([head, jnp.zeros((32, order - 32), F32)], axis=1),
            jnp.concatenate([lower, rest], axis=1),
        ],
        axis=0,
    )


def joined(top, edge, corner):
    return jnp.concatenate(
        [jnp.concatenate([top, edge.T], axis=1), jnp.concatenate([edge, corner], axis=1)], axis=0
    )


def small_start(gram):
    inverse = block_inverse(symmetric(gram[:, :32]))
    return inverse, symmetric(against(mul(inverse, symmetric(gram[:, 32:])), inverse))


def small_step(known, known_images, origin, gram, image_part):
    edge = known.shape[0]
    order = edge + 32
    seen = origin.shape[1]
    basis_gram = joined(known, gram[:, :edge], symmetric(gram[:, edge:order]))
    cross_images = 0.5 * (gram[:, order:] + against(image_part[:, :seen], origin))
    image_gram = joined(known_images, cross_images, symmetric(image_part[:, seen:]))
    head = lax.broadcasted_iota(jnp.int32, (1, order), 1) < 32
    down = lax.broadcasted_iota(jnp.int32, (order, 1), 0) < 32
    diagonal = basis_gram * unit(order)
    scale = jnp.where(head, 1.0, lax.rsqrt(jnp.sum(diagonal, axis=0, keepdims=True) + EPSILON))
    scale_down = jnp.where(down, 1.0, lax.rsqrt(jnp.sum(diagonal, axis=1, keepdims=True) + EPSILON))
    basis_gram = scale_down * basis_gram * scale
    image_gram = scale_down * image_gram * scale
    cross = basis_gram[32:, :32]
    tail = factor_inverse(basis_gram[32:, 32:] - against(cross, cross))
    inverse = jnp.concatenate(
        [
            jnp.concatenate([unit(32), jnp.zeros((32, edge), F32)], axis=1),
            jnp.concatenate([-mul(tail, cross), tail], axis=1),
        ],
        axis=0,
    )
    reduced = symmetric(against(mul(inverse, image_gram), inverse))
    size = jnp.sqrt(jnp.sum(jnp.sum(reduced * reduced, axis=1, keepdims=True), axis=0, keepdims=True))
    filtered = (reduced + size * unit(order)) / (2.0 * size)
    filtered = mul(filtered, filtered)
    leading = mul(filtered, filtered[:, :32])
    turned = mul(block_inverse(mul_left(leading, leading)), leading.T)
    weights = mul(turned, inverse)
    weights = jnp.concatenate([weights, jnp.where(head, 0.0, weights)], axis=0)
    next_basis = symmetric(against(mul(weights, basis_gram), weights))
    next_images = symmetric(against(mul(weights, image_gram), weights))
    weights = weights * scale
    next_origin = jnp.concatenate([mul(weights[:, :edge], origin), weights[:, edge:]], axis=1)
    return weights, next_basis, next_images, next_origin


def algebra_kernel(first, *refs):
    if first:
        gram, weights_out, ritz_out = refs
        weights_out[...], ritz_out[...] = small_start(gram[...])
        return
    width = 2 * refs[0].shape[0] + 32
    known, known_images, origin, gram = (r[...] for r in refs[:4])
    results = small_step(known, known_images, origin, gram[:, :width], gram[:, width:])
    for out, value in zip(refs[4:], results):
        out[...] = value


def algebra(gram, known):
    if not known:
        shapes = [(32, 32), (32, 32)]
    else:
        shapes = [(64, known[0].shape[0] + 32), (64, 64), (64, 64), (64, known[2].shape[1] + 32)]
    return pl.pallas_call(
        functools.partial(algebra_kernel, not known),
        out_shape=[jax.ShapeDtypeStruct(s, F32) for s in shapes],
        compiler_params=params(),
        cost_estimate=pl.CostEstimate(flops=1 << 28, bytes_accessed=20 << 20, transcendentals=0),
    )(*known, gram)


def update_kernel(n, *refs):
    basis, images, terms = refs[:n], refs[n : 2 * n - 1], refs[2 * n - 1 : 2 * n + 3]
    mask, weights, ritz = refs[2 * n + 3], refs[2 * n + 4][...], refs[2 * n + 5][:32, :32]
    outs = refs[2 * n + 6 :]
    for t in range(4):
        newest = ((terms[0][t] + terms[1][t]) + (terms[2][t] + terms[3][t])) * mask[t]
        moved = mul(weights, jnp.concatenate([b[t] for b in basis], axis=0))
        moved_images = mul(weights, jnp.concatenate([b[t] for b in images] + [newest], axis=0))
        residual = moved_images[:32] - mul(ritz, moved[:32])
        outs[0][t] = (residual * mask[t]).astype(BF16)
        outs[1][t] = residual
        outs[2][t] = moved[:32]
        outs[3][t] = moved_images[:32]
        if n > 1:
            outs[4][t] = moved[32:]
            outs[5][t] = moved_images[32:]


def update(basis, images, terms, mask, weights, ritz):
    n = len(basis)
    slab = jax.ShapeDtypeStruct((4, 32, 256), F32)
    return pl.pallas_call(
        functools.partial(update_kernel, n),
        out_shape=[jax.ShapeDtypeStruct((4, 32, 256), BF16)] + [slab] * (3 if n == 1 else 5),
        compiler_params=params(),
        cost_estimate=pl.CostEstimate(flops=1 << 27, bytes_accessed=1 << 20, transcendentals=0),
    )(*basis, *images, *terms, mask, weights, ritz)


def finish_kernel(n, *refs):
    basis, weights, out = refs[:n], refs[n][:32], refs[n + 1]
    for t in range(4):
        out[t] = mul(weights, jnp.concatenate([b[t] for b in basis], axis=0))


def finish(basis, weights):
    return pl.pallas_call(
        functools.partial(finish_kernel, len(basis)),
        out_shape=jax.ShapeDtypeStruct((4, 32, 256), F32),
        compiler_params=params(),
    )(*basis, weights)


def body(x_start, bin_mask, band, off_tiles, off_rows, off_cols, off_count):
    width = x_start.shape[1]
    band = band[:, 0]
    tiles = off_tiles[0, 0]
    row_ids, col_ids = off_rows[0, 0], off_cols[0, 0]
    ids = jnp.stack(
        [lax.axis_index("brow"), lax.axis_index("bcol"), off_count[0, 0], jnp.int32(0)]
    ).astype(jnp.int32)
    mask = bin_mask.astype(F32).reshape(4, 1, 256)
    started = x_start.T.reshape(width, 4, 256).transpose(1, 0, 2) * mask

    gathered = []

    def apply_operator(packed, plain, last=False):
        pair = jnp.stack([packed, flip(packed, "bcol", 2)])
        near = [pair] + [flip(pair, "bcol", 4 * k) for k in (1, 2, 3)]
        across = [flip(part, "bcol", 1) for part in near]
        col_pair = jnp.stack([packed, flip(packed, "brow", 4)])
        along = [col_pair] + [flip(col_pair, "brow", k) for k in (1, 2, 3)]
        rows, rim, cols = assemble(ids, near + across + along)
        limit = VMEM_BYTES if gathered else STREAM_BYTES
        spread, spill = band_back(ids, band, rows, limit)
        if not last:
            rim, spill, spread = lax.optimization_barrier((rim, spill, spread))
            spilled = shifted(spill, "brow", 1)
        rim = shifted(rim, "brow", -1)
        gathered.append((rows, cols, rim))
        away, col_all, *col_sums = far(ids, row_ids, col_ids, tiles, rows, cols, limit)
        same, other = band_forward(ids, band, rows, rim, spread, away)
        image_part = image_grams(ids, same, other, col_all, spread, gathered)
        gram = sum_all(jnp.concatenate([plain, image_part], axis=1))
        if last:
            return gram, None
        other, spilled = lax.optimization_barrier((other, spilled))
        arrived = flip(other, "bcol", 1)
        folded = fold(ids, same, arrived, spilled, flip(spilled[1], "bcol", 1))
        folded, col_sums = lax.optimization_barrier((folded, col_sums))
        c0, c1, c2, c3 = [col_sums[0]] + [
            flip(col_sums[k], "brow", k).astype(F32) for k in (1, 2, 3)
        ]
        col_total = (c0 + c1) + (c2 + c3)
        col_other = flip(col_total[1], "brow", 4)
        r0, r1, r2, r3 = [folded[0]] + [
            flip(folded[k], "bcol", 4 * k).astype(F32) for k in (1, 2, 3)
        ]
        row_total = (r0 + r1) + (r2 + r3)
        row_other = flip(row_total[1], "bcol", 2)
        return gram, [row_total[0], row_other, col_total[0], col_other]

    gram, terms = apply_operator((started * mask).astype(BF16), grams([], [], started))
    weights, ritz = algebra(gram, [])
    known = [jnp.eye(width, dtype=F32), ritz, weights]
    packed, residual, vectors, images = update([started], [], terms, mask, weights, ritz)
    older, older_images = [vectors], [images]
    for step in range(STEPS):
        last = step == STEPS - 1
        gram, terms = apply_operator(packed, grams(older, older_images, residual), last)
        weights, *known = algebra(gram, known)
        basis = older + [residual]
        if not last:
            packed, residual, vectors, images, tail, tail_images = update(
                basis, older_images, terms, mask, weights, known[1]
            )
            older, older_images = [vectors, tail], [images, tail_images]
    vectors = finish(basis, weights)
    return vectors.transpose(1, 0, 2).reshape(width, -1).T, known[1][:width, :width]


def solution(mesh):
    return jax.shard_map(
        body,
        mesh=mesh,
        in_specs=(
            P(("brow", "bcol"), None),
            P(("brow", "bcol")),
            P("brow", "bcol", None, None),
            P("brow", "bcol", None, None, None),
            P("brow", "bcol", None),
            P("brow", "bcol", None),
            P("brow", "bcol"),
        ),
        out_specs=(P(("brow", "bcol"), None), P()),
        check_vma=False,
    )
```

```python
import functools

import jax
import jax.numpy as jnp
from jax import lax
from jax.experimental import pallas as pl
from jax.experimental.pallas import tpu as pltpu
from jax.sharding import PartitionSpec as P

STEPS = 3
PRECISE = lax.Precision.HIGHEST
EPSILON = 1e-06
F32 = jnp.float32
BF16 = jnp.bfloat16
GROUP = 16
VMEM_BYTES = 24 * 1024 * 1024
PAIR = (2, 4, 32, 256)


def flip(value, axis, by):
    length = lax.axis_size(axis)
    return lax.ppermute(value, axis, [(i, i ^ by) for i in range(length)])


def flip_both(value, row_by, col_by):
    rows, cols = lax.axis_size("brow"), lax.axis_size("bcol")
    pairs = [
        (r * cols + c, (r ^ row_by) * cols + (c ^ col_by)) for r in range(rows) for c in range(cols)
    ]
    return lax.ppermute(value, ("brow", "bcol"), pairs)


def shifted(value, axis, by):
    length = lax.axis_size(axis)
    pairs = [(i, i + by) for i in range(length) if 0 <= i + by < length]
    return lax.ppermute(value, axis, pairs)


def sum_all(value):
    value = value + flip(value, "bcol", 1)
    value = (value + flip(value, "bcol", 4)) + (flip(value, "bcol", 8) + flip(value, "bcol", 12))
    value = (value + flip(value, "brow", 1)) + (flip(value, "brow", 2) + flip(value, "brow", 3))
    value = (value + flip(value, "bcol", 2)) + (flip(value, "brow", 4) + flip_both(value, 4, 2))
    return value


def whole(shape):
    return pl.BlockSpec(shape, lambda *_: (0,) * len(shape))


def params():
    return pltpu.CompilerParams(vmem_limit_bytes=VMEM_BYTES)


def assemble_kernel(ids, p0, p1, p2, p3, q0, q1, q2, q3, c0, c1, c2, c3, rows_out, rim_out, cols_out):
    mine, me = ids[0], ids[1]
    near, across, along = (p0, p1, p2, p3), (q0, q1, q2, q3), (c0, c1, c2, c3)
    for k in range(4):
        for half in range(2):
            for parity, refs in ((0, near), (1, across)):
                slab = me ^ (4 * k + 2 * half + parity)
                rows_out[pl.ds(4 * slab, 4)] = refs[k][half]
            slab = mine ^ (4 * half + k)
            cols_out[pl.ds(4 * slab, 4)] = along[k][half]
    rim_out[...] = rows_out[:16]


def assemble(ids, parts):
    return pl.pallas_call(
        assemble_kernel,
        grid_spec=pltpu.PrefetchScalarGridSpec(
            num_scalar_prefetch=1,
            grid=(1,),
            in_specs=[whole((2, 4, 32, 256))] * 12,
            out_specs=[whole((64, 32, 256)), whole((16, 32, 256)), whole((32, 32, 256))],
        ),
        out_shape=[
            jax.ShapeDtypeStruct((64, 32, 256), BF16),
            jax.ShapeDtypeStruct((16, 32, 256), BF16),
            jax.ShapeDtypeStruct((32, 32, 256), BF16),
        ],
        compiler_params=params(),
        cost_estimate=pl.CostEstimate(flops=0, bytes_accessed=3 << 20, transcendentals=0),
    )(ids, *parts)


def back_kernel(ids, band, rows, spread, spill):
    me = ids[1]
    step = pl.program_id(0)

    @pl.when(step == 0)
    def _():
        spread[:16] = jnp.zeros((16, 32, 256), F32)
        spread[64:] = jnp.zeros((16, 32, 256), F32)

    first = step * GROUP
    products = [
        jnp.dot(rows[first + g], band[g], preferred_element_type=F32) for g in range(GROUP)
    ]
    for g in range(GROUP):
        spread[first + g + me] = products[g]

    @pl.when(step == pl.num_programs(0) - 1)
    def _():
        for half in range(2):
            for parity in range(2):
                slab = (me & 3) ^ (2 * half + parity)
                spill[parity, half] = spread[pl.ds(64 + 4 * slab, 4)].astype(BF16)


def band_back(ids, band, rows):
    return pl.pallas_call(
        back_kernel,
        grid_spec=pltpu.PrefetchScalarGridSpec(
            num_scalar_prefetch=1,
            grid=(64 // GROUP,),
            in_specs=[
                pl.BlockSpec((GROUP, 256, 256), lambda i, *_: (i, 0, 0)),
                whole((64, 32, 256)),
            ],
            out_specs=[whole((80, 32, 256)), whole((2,) + PAIR)],
        ),
        out_shape=[
            jax.ShapeDtypeStruct((80, 32, 256), F32),
            jax.ShapeDtypeStruct((2,) + PAIR, BF16),
        ],
        compiler_params=params(),
        cost_estimate=pl.CostEstimate(
            flops=2 * 64 * 256 * 256 * 32, bytes_accessed=11 << 20, transcendentals=0
        ),
    )(ids, band, rows)


def far_kernel(ids, row_ids, col_ids, tiles, rows, cols, out, acc, k0, k1, k2, k3):
    mine, count = ids[0], ids[2]
    step = pl.program_id(0)

    @pl.when(step == 0)
    def _():
        out[...] = jnp.zeros_like(out)
        acc[...] = jnp.zeros_like(acc)

    def visit(base_slot, partial):
        first = step * GROUP + base_slot
        found = []
        for g in range(8):
            i = first + g
            live = i < count
            a, b = row_ids[i], col_ids[i]
            if partial:
                a, b = jnp.where(live, a, 0), jnp.where(live, b, 0)
            tile = tiles[base_slot + g]
            forward = lax.dot_general(
                cols[b], tile, (((1,), (1,)), ((), ())), preferred_element_type=F32
            )
            back = jnp.dot(rows[a], tile, preferred_element_type=F32)
            if partial:
                forward, back = jnp.where(live, forward, 0.0), jnp.where(live, back, 0.0)
            found.append((a, b, forward, back))
        for a, b, forward, back in found:
            out[a] += forward
            acc[b] += back

    for h in range(0, GROUP, 8):
        first = step * GROUP + h

        @pl.when(first + 8 <= count)
        def _():
            visit(h, False)

        @pl.when((first + 8 > count) & (first < count))
        def _():
            visit(h, True)

    @pl.when(step == pl.num_programs(0) - 1)
    def _():
        for j in range(8):
            piece = acc[pl.ds(4 * (mine ^ j), 4)]
            target = (k0, k1, k2, k3)[j & 3]
            target[j >> 2] = piece.astype(target.dtype)


def pair_shapes():
    return [jax.ShapeDtypeStruct(PAIR, F32)] + [jax.ShapeDtypeStruct(PAIR, BF16)] * 3


def far(ids, row_ids, col_ids, tiles, rows, cols):
    return pl.pallas_call(
        far_kernel,
        grid_spec=pltpu.PrefetchScalarGridSpec(
            num_scalar_prefetch=3,
            grid=(64 // GROUP,),
            in_specs=[
                pl.BlockSpec((GROUP, 256, 256), lambda i, *_: (i, 0, 0)),
                whole((64, 32, 256)),
                whole((32, 32, 256)),
            ],
            out_specs=[whole((64, 32, 256)), whole((32, 32, 256))] + [whole(PAIR)] * 4,
        ),
        out_shape=[
            jax.ShapeDtypeStruct((64, 32, 256), F32),
            jax.ShapeDtypeStruct((32, 32, 256), F32),
        ]
        + pair_shapes(),
        compiler_params=params(),
        cost_estimate=pl.CostEstimate(
            flops=4 * 64 * 256 * 256 * 32, bytes_accessed=15 << 20, transcendentals=0
        ),
    )(ids, row_ids, col_ids, tiles, rows, cols)


def forward_kernel(ids, band, rows, rim, spread, away, same, other, extended, halves):
    me = ids[1]
    step = pl.program_id(0)

    @pl.when(step == 0)
    def _():
        extended[:64] = rows[...]
        extended[64:80] = rim[...]

    first = step * GROUP
    products = [
        lax.dot_general(
            extended[first + g + me], band[g], (((1,), (1,)), ((), ())), preferred_element_type=F32
        )
        + (spread[g] + away[g])
        for g in range(GROUP)
    ]
    for h in range(GROUP // 4):
        slot = me ^ (step * (GROUP // 4) + h)
        for t in range(4):
            halves[slot & 1, slot >> 1, t] = products[4 * h + t]

    @pl.when(step == pl.num_programs(0) - 1)
    def _():
        same[...] = halves[0]
        other[...] = halves[1]


def band_forward(ids, band, rows, rim, spread, away):
    return pl.pallas_call(
        forward_kernel,
        grid_spec=pltpu.PrefetchScalarGridSpec(
            num_scalar_prefetch=1,
            grid=(64 // GROUP,),
            in_specs=[
                pl.BlockSpec((GROUP, 256, 256), lambda i, *_: (i, 0, 0)),
                whole((64, 32, 256)),
                whole((16, 32, 256)),
                pl.BlockSpec((GROUP, 32, 256), lambda i, *_: (i, 0, 0)),
                pl.BlockSpec((GROUP, 32, 256), lambda i, *_: (i, 0, 0)),
            ],
            out_specs=[whole((8, 4, 32, 256))] * 2,
            scratch_shapes=[
                pltpu.VMEM((80, 32, 256), BF16),
                pltpu.VMEM((2, 8, 4, 32, 256), F32),
            ],
        ),
        out_shape=[jax.ShapeDtypeStruct((8, 4, 32, 256), F32)] * 2,
        compiler_params=params(),
        cost_estimate=pl.CostEstimate(
            flops=0, bytes_accessed=1 << 16, transcendentals=0
        ),
    )(ids, band, rows, rim, spread, away)


def fold_kernel(ids, same, arrived, spilled, spilled_across, *outs):
    here = ids[1] >> 2
    extra = spilled[0].astype(F32) + spilled_across[...].astype(F32)
    for k in range(4):
        total = same[2 * k : 2 * k + 2] + arrived[2 * k : 2 * k + 2]
        total = total + jnp.where(here == k, extra, 0.0)
        outs[k][...] = total.astype(outs[k].dtype)


def fold(ids, same, arrived, spilled, spilled_across):
    return pl.pallas_call(
        fold_kernel,
        grid_spec=pltpu.PrefetchScalarGridSpec(
            num_scalar_prefetch=1,
            grid=(1,),
            in_specs=[whole((8, 4, 32, 256)), whole((8, 4, 32, 256)), whole((2,) + PAIR), whole(PAIR)],
            out_specs=[whole(PAIR)] * 4,
        ),
        out_shape=pair_shapes(),
        compiler_params=params(),
        cost_estimate=pl.CostEstimate(flops=0, bytes_accessed=3 << 20, transcendentals=0),
    )(ids, same, arrived, spilled, spilled_across)


def against(left, right):
    return lax.dot_general(
        left, right, (((1,), (1,)), ((), ())), precision=PRECISE, preferred_element_type=F32
    )


def image_gram_kernel(n, ids, same, other, cols, spread, *refs):
    evens, odds, alongs, rims, out = refs[:n], refs[n : 2 * n], refs[2 * n : 3 * n], refs[3 * n : 4 * n], refs[-1]

    @pl.when(pl.program_id(0) == 0)
    def _():
        out[...] = jnp.zeros_like(out)

    total = jnp.zeros((32, 32 * n), F32)
    jobs = [(same.at[0], [r.at[0] for r in evens], 4), (other.at[0], [r.at[0] for r in odds], 4)]
    jobs += [(cols, alongs, 4), (spread, rims, 2)]
    for part, known, count in jobs:
        for t in range(count):
            columns = jnp.concatenate([k[t] for k in known], axis=0)
            total += lax.dot_general(
                part[t].astype(BF16), columns, (((1,), (1,)), ((), ())), preferred_element_type=F32
            )
    out[...] += total


def image_grams(ids, same, other, cols, spread, gathered):
    n = len(gathered)
    slab = (1, 4, 32, 256)
    at_even = pl.BlockSpec(slab, lambda e, ids: (ids[1] ^ (2 * e), 0, 0, 0))
    at_odd = pl.BlockSpec(slab, lambda e, ids: (ids[1] ^ (2 * e + 1), 0, 0, 0))
    at_slab = pl.BlockSpec(slab, lambda e, ids: (e, 0, 0, 0))
    four = pl.BlockSpec((4, 32, 256), lambda e, ids: (e, 0, 0))
    two = pl.BlockSpec((2, 32, 256), lambda e, ids: (e, 0, 0))
    over = pl.BlockSpec((2, 32, 256), lambda e, ids: (32 + e, 0, 0))
    rows = [g[0].reshape(16, 4, 32, 256) for g in gathered]
    return pl.pallas_call(
        functools.partial(image_gram_kernel, n),
        grid_spec=pltpu.PrefetchScalarGridSpec(
            num_scalar_prefetch=1,
            grid=(8,),
            in_specs=[at_slab, at_slab, four, over]
            + [at_even] * n
            + [at_odd] * n
            + [four] * n
            + [two] * n,
            out_specs=whole((32, 32 * n)),
        ),
        out_shape=jax.ShapeDtypeStruct((32, 32 * n), F32),
        compiler_params=params(),
        cost_estimate=pl.CostEstimate(flops=1 << 28, bytes_accessed=8 << 20, transcendentals=0),
    )(ids, same, other, cols, spread, *rows, *rows, *[g[1] for g in gathered], *[g[2] for g in gathered])


def gram_kernel(n, *refs):
    basis, images, out = refs[: n + 1], refs[n + 1 : 2 * n + 1], refs[-1]
    total = jnp.zeros((32, 32 * (2 * n + 1)), F32)
    for t in range(4):
        columns = jnp.concatenate([b[t] for b in basis] + [b[t] for b in images], axis=0)
        total += against(basis[-1][t], columns)
    out[...] = total


def grams(older, older_images, newest):
    n = len(older)
    return pl.pallas_call(
        functools.partial(gram_kernel, n),
        out_shape=jax.ShapeDtypeStruct((32, 32 * (2 * n + 1)), F32),
        compiler_params=params(),
        cost_estimate=pl.CostEstimate(flops=1 << 27, bytes_accessed=1 << 20, transcendentals=0),
    )(*older, newest, *older_images)


def mul(left, right):
    return jnp.dot(left, right, precision=PRECISE, preferred_element_type=F32)


def mul_left(left, right):
    return lax.dot_general(
        left, right, (((0,), (0,)), ((), ())), precision=PRECISE, preferred_element_type=F32
    )


def symmetric(matrix):
    return 0.5 * (matrix + matrix.T)


def unit(order):
    return (
        lax.broadcasted_iota(jnp.int32, (order, order), 0)
        == lax.broadcasted_iota(jnp.int32, (order, order), 1)
    ).astype(F32)


def block_inverse(matrix):
    order = matrix.shape[0]
    table = jnp.concatenate([matrix, unit(order)], axis=1)
    places = lax.broadcasted_iota(jnp.int32, (order, 2 * order), 0)
    for k in range(0, order, 2):
        left = jnp.broadcast_to(table[:, k : k + 1], table.shape)
        right = jnp.broadcast_to(table[:, k + 1 : k + 2], table.shape)
        inverse = 1.0 / left[k : k + 1]
        share = right[k : k + 1] * inverse
        top = table[k : k + 1] * inverse
        corner = right[k + 1 : k + 2] - share * right[k : k + 1]
        second = (table[k + 1 : k + 2] - share * table[k : k + 1]) / corner
        table = (
            table
            - jnp.where(places > k, left, 0.0) * top
            - jnp.where(places > k + 1, right - left * share, 0.0) * second
        )
    pivots = jnp.sum(table[:, :order] * unit(order), axis=1, keepdims=True)
    return table[:, order:] * lax.rsqrt(pivots)


def factor_inverse(matrix):
    order = matrix.shape[0]
    if order == 32:
        return block_inverse(matrix)
    head = block_inverse(matrix[:32, :32])
    edge = mul(head, matrix[:32, 32:])
    rest = factor_inverse(matrix[32:, 32:] - mul_left(edge, edge))
    lower = -mul(rest, mul_left(edge, head))
    return jnp.concatenate(
        [
            jnp.concatenate([head, jnp.zeros((32, order - 32), F32)], axis=1),
            jnp.concatenate([lower, rest], axis=1),
        ],
        axis=0,
    )


def joined(top, edge, corner):
    return jnp.concatenate(
        [jnp.concatenate([top, edge.T], axis=1), jnp.concatenate([edge, corner], axis=1)], axis=0
    )


def small_start(gram):
    inverse = block_inverse(symmetric(gram[:, :32]))
    return inverse, symmetric(against(mul(inverse, symmetric(gram[:, 32:])), inverse))


def small_step(known, known_images, origin, gram, image_part, last):
    edge = known.shape[0]
    order = edge + 32
    seen = origin.shape[1]
    basis_gram = joined(known, gram[:, :edge], symmetric(gram[:, edge:order]))
    cross_images = 0.5 * (gram[:, order:] + against(image_part[:, :seen], origin))
    image_gram = joined(known_images, cross_images, symmetric(image_part[:, seen:]))
    head = lax.broadcasted_iota(jnp.int32, (1, order), 1) < 32
    down = lax.broadcasted_iota(jnp.int32, (order, 1), 0) < 32
    diagonal = basis_gram * unit(order)
    scale = jnp.where(head, 1.0, lax.rsqrt(jnp.sum(diagonal, axis=0, keepdims=True) + EPSILON))
    scale_down = jnp.where(down, 1.0, lax.rsqrt(jnp.sum(diagonal, axis=1, keepdims=True) + EPSILON))
    basis_gram = scale_down * basis_gram * scale
    image_gram = scale_down * image_gram * scale
    cross = basis_gram[32:, :32]
    tail = factor_inverse(basis_gram[32:, 32:] - against(cross, cross))
    inverse = jnp.concatenate(
        [
            jnp.concatenate([unit(32), jnp.zeros((32, edge), F32)], axis=1),
            jnp.concatenate([-mul(tail, cross), tail], axis=1),
        ],
        axis=0,
    )
    reduced = symmetric(against(mul(inverse, image_gram), inverse))
    size = jnp.sqrt(jnp.sum(jnp.sum(reduced * reduced, axis=1, keepdims=True), axis=0, keepdims=True))
    filtered = (reduced + size * unit(order)) / (2.0 * size)
    filtered = mul(filtered, filtered)
    leading = mul(filtered, filtered[:, :32])
    turned = mul(block_inverse(mul_left(leading, leading)), leading.T)
    weights = mul(turned, inverse)
    if last:
        return weights * scale, symmetric(against(mul(weights, image_gram), weights))
    weights = jnp.concatenate([weights, jnp.where(head, 0.0, weights)], axis=0)
    next_basis = symmetric(against(mul(weights, basis_gram), weights))
    next_images = symmetric(against(mul(weights, image_gram), weights))
    weights = weights * scale
    next_origin = jnp.concatenate([mul(weights[:, :edge], origin), weights[:, edge:]], axis=1)
    return weights, next_basis, next_images, next_origin


def algebra_kernel(first, last, *refs):
    if first:
        gram, weights_out, ritz_out = refs
        weights_out[...], ritz_out[...] = small_start(gram[...])
        return
    width = 2 * refs[0].shape[0] + 32
    known, known_images, origin, gram = (r[...] for r in refs[:4])
    results = small_step(known, known_images, origin, gram[:, :width], gram[:, width:], last)
    for out, value in zip(refs[4:], results):
        out[...] = value


def algebra(gram, known, last=False):
    if not known:
        shapes = [(32, 32), (32, 32)]
    elif last:
        shapes = [(32, known[0].shape[0] + 32), (32, 32)]
    else:
        shapes = [(64, known[0].shape[0] + 32), (64, 64), (64, 64), (64, known[2].shape[1] + 32)]
    return pl.pallas_call(
        functools.partial(algebra_kernel, not known, last),
        out_shape=[jax.ShapeDtypeStruct(s, F32) for s in shapes],
        compiler_params=params(),
        cost_estimate=pl.CostEstimate(flops=1 << 28, bytes_accessed=20 << 20, transcendentals=0),
    )(*known, gram)


def update_kernel(n, *refs):
    basis, images, terms = refs[:n], refs[n : 2 * n - 1], refs[2 * n - 1 : 2 * n + 3]
    mask, weights, ritz = refs[2 * n + 3], refs[2 * n + 4][...], refs[2 * n + 5][:32, :32]
    outs = refs[2 * n + 6 :]
    for t in range(4):
        newest = ((terms[0][t] + terms[1][t]) + (terms[2][t] + terms[3][t])) * mask[t]
        moved = mul(weights, jnp.concatenate([b[t] for b in basis], axis=0))
        moved_images = mul(weights, jnp.concatenate([b[t] for b in images] + [newest], axis=0))
        residual = moved_images[:32] - mul(ritz, moved[:32])
        outs[0][t] = (residual * mask[t]).astype(BF16)
        outs[1][t] = residual
        outs[2][t] = moved[:32]
        outs[3][t] = moved_images[:32]
        if n > 1:
            outs[4][t] = moved[32:]
            outs[5][t] = moved_images[32:]


def update(basis, images, terms, mask, weights, ritz):
    n = len(basis)
    slab = jax.ShapeDtypeStruct((4, 32, 256), F32)
    return pl.pallas_call(
        functools.partial(update_kernel, n),
        out_shape=[jax.ShapeDtypeStruct((4, 32, 256), BF16)] + [slab] * (3 if n == 1 else 5),
        compiler_params=params(),
        cost_estimate=pl.CostEstimate(flops=1 << 27, bytes_accessed=1 << 20, transcendentals=0),
    )(*basis, *images, *terms, mask, weights, ritz)


def finish_kernel(n, *refs):
    basis, weights, out = refs[:n], refs[n][...], refs[n + 1]
    for t in range(4):
        out[t] = mul(weights, jnp.concatenate([b[t] for b in basis], axis=0))


def finish(basis, weights):
    return pl.pallas_call(
        functools.partial(finish_kernel, len(basis)),
        out_shape=jax.ShapeDtypeStruct((4, 32, 256), F32),
        compiler_params=params(),
    )(*basis, weights)


def body(x_start, bin_mask, band, off_tiles, off_rows, off_cols, off_count):
    width = x_start.shape[1]
    band = band[:, 0]
    tiles = off_tiles[0, 0]
    row_ids, col_ids = off_rows[0, 0], off_cols[0, 0]
    ids = jnp.stack(
        [lax.axis_index("brow"), lax.axis_index("bcol"), off_count[0, 0], jnp.int32(0)]
    ).astype(jnp.int32)
    mask = bin_mask.astype(F32).reshape(4, 1, 256)
    started = x_start.T.reshape(width, 4, 256).transpose(1, 0, 2) * mask

    gathered = []

    def apply_operator(packed, plain, last=False):
        pair = jnp.stack([packed, flip(packed, "bcol", 2)])
        near = [pair] + [flip(pair, "bcol", 4 * k) for k in (1, 2, 3)]
        across = [flip(part, "bcol", 1) for part in near]
        col_pair = jnp.stack([packed, flip(packed, "brow", 4)])
        along = [col_pair] + [flip(col_pair, "brow", k) for k in (1, 2, 3)]
        rows, rim, cols = assemble(ids, near + across + along)
        spread, spill = band_back(ids, band, rows)
        if not last:
            rim, spill, spread = lax.optimization_barrier((rim, spill, spread))
            spilled = shifted(spill, "brow", 1)
        rim = shifted(rim, "brow", -1)
        gathered.append((rows, cols, rim))
        away, col_all, *col_sums = far(ids, row_ids, col_ids, tiles, rows, cols)
        same, other = band_forward(ids, band, rows, rim, spread, away)
        image_part = image_grams(ids, same, other, col_all, spread, gathered)
        gram = sum_all(jnp.concatenate([plain, image_part], axis=1))
        if last:
            return gram, None
        other, spilled = lax.optimization_barrier((other, spilled))
        arrived = flip(other, "bcol", 1)
        folded = fold(ids, same, arrived, spilled, flip(spilled[1], "bcol", 1))
        folded, col_sums = lax.optimization_barrier((folded, col_sums))
        c0, c1, c2, c3 = [col_sums[0]] + [
            flip(col_sums[k], "brow", k).astype(F32) for k in (1, 2, 3)
        ]
        col_total = (c0 + c1) + (c2 + c3)
        col_other = flip(col_total[1], "brow", 4)
        r0, r1, r2, r3 = [folded[0]] + [
            flip(folded[k], "bcol", 4 * k).astype(F32) for k in (1, 2, 3)
        ]
        row_total = (r0 + r1) + (r2 + r3)
        row_other = flip(row_total[1], "bcol", 2)
        return gram, [row_total[0], row_other, col_total[0], col_other]

    gram, terms = apply_operator((started * mask).astype(BF16), grams([], [], started))
    weights, ritz = algebra(gram, [])
    known = [jnp.eye(width, dtype=F32), ritz, weights]
    packed, residual, vectors, images = update([started], [], terms, mask, weights, ritz)
    older, older_images = [vectors], [images]
    for step in range(STEPS):
        last = step == STEPS - 1
        gram, terms = apply_operator(packed, grams(older, older_images, residual), last)
        weights, *known = algebra(gram, known, last)
        basis = older + [residual]
        if not last:
            packed, residual, vectors, images, tail, tail_images = update(
                basis, older_images, terms, mask, weights, known[1]
            )
            older, older_images = [vectors, tail], [images, tail_images]
    vectors = finish(basis, weights)
    return vectors.transpose(1, 0, 2).reshape(width, -1).T, known[0]


def solution(mesh):
    return jax.shard_map(
        body,
        mesh=mesh,
        in_specs=(
            P(("brow", "bcol"), None),
            P(("brow", "bcol")),
            P("brow", "bcol", None, None),
            P("brow", "bcol", None, None, None),
            P("brow", "bcol", None),
            P("brow", "bcol", None),
            P("brow", "bcol"),
        ),
        out_specs=(P(("brow", "bcol"), None), P()),
        check_vma=False,
    )
```

```python
import functools

import jax
import jax.numpy as jnp
from jax import lax
from jax.experimental import pallas as pl
from jax.experimental.pallas import tpu as pltpu
from jax.sharding import PartitionSpec as P

STEPS = 3
PRECISE = lax.Precision.HIGHEST
EPSILON = 1e-06
F32 = jnp.float32
BF16 = jnp.bfloat16
GROUP = 16
VMEM_BYTES = 24 * 1024 * 1024
PAIR = (2, 4, 32, 256)


def flip(value, axis, by):
    length = lax.axis_size(axis)
    return lax.ppermute(value, axis, [(i, i ^ by) for i in range(length)])


def flip_both(value, row_by, col_by):
    rows, cols = lax.axis_size("brow"), lax.axis_size("bcol")
    pairs = [
        (r * cols + c, (r ^ row_by) * cols + (c ^ col_by)) for r in range(rows) for c in range(cols)
    ]
    return lax.ppermute(value, ("brow", "bcol"), pairs)


def shifted(value, axis, by):
    length = lax.axis_size(axis)
    pairs = [(i, i + by) for i in range(length) if 0 <= i + by < length]
    return lax.ppermute(value, axis, pairs)


def sum_all(value):
    value = value + flip(value, "bcol", 1)
    value = (value + flip(value, "bcol", 4)) + (flip(value, "bcol", 8) + flip(value, "bcol", 12))
    value = (value + flip(value, "brow", 1)) + (flip(value, "brow", 2) + flip(value, "brow", 3))
    value = (value + flip(value, "bcol", 2)) + (flip(value, "brow", 4) + flip_both(value, 4, 2))
    return value


def whole(shape):
    return pl.BlockSpec(shape, lambda *_: (0,) * len(shape))


def params():
    return pltpu.CompilerParams(vmem_limit_bytes=VMEM_BYTES)


def assemble_kernel(ids, p0, p1, p2, p3, q0, q1, q2, q3, c0, c1, c2, c3, rows_out, rim_out, cols_out):
    mine, me = ids[0], ids[1]
    near, across, along = (p0, p1, p2, p3), (q0, q1, q2, q3), (c0, c1, c2, c3)
    for k in range(4):
        for half in range(2):
            for parity, refs in ((0, near), (1, across)):
                slab = me ^ (4 * k + 2 * half + parity)
                rows_out[pl.ds(4 * slab, 4)] = refs[k][half]
            slab = mine ^ (4 * half + k)
            cols_out[pl.ds(4 * slab, 4)] = along[k][half]
    rim_out[...] = rows_out[:16]


def assemble(ids, parts):
    return pl.pallas_call(
        assemble_kernel,
        grid_spec=pltpu.PrefetchScalarGridSpec(
            num_scalar_prefetch=1,
            grid=(1,),
            in_specs=[whole((2, 4, 32, 256))] * 12,
            out_specs=[whole((64, 32, 256)), whole((16, 32, 256)), whole((32, 32, 256))],
        ),
        out_shape=[
            jax.ShapeDtypeStruct((64, 32, 256), BF16),
            jax.ShapeDtypeStruct((16, 32, 256), BF16),
            jax.ShapeDtypeStruct((32, 32, 256), BF16),
        ],
        compiler_params=params(),
        cost_estimate=pl.CostEstimate(flops=0, bytes_accessed=3 << 20, transcendentals=0),
    )(ids, *parts)


def back_kernel(ids, band, rows, spread, spill):
    me = ids[1]
    step = pl.program_id(0)

    @pl.when(step == 0)
    def _():
        spread[:16] = jnp.zeros((16, 32, 256), F32)
        spread[64:] = jnp.zeros((16, 32, 256), F32)

    first = step * GROUP
    products = [
        jnp.dot(rows[first + g], band[g], preferred_element_type=F32) for g in range(GROUP)
    ]
    for g in range(GROUP):
        spread[first + g + me] = products[g]

    @pl.when(step == pl.num_programs(0) - 1)
    def _():
        for half in range(2):
            for parity in range(2):
                slab = (me & 3) ^ (2 * half + parity)
                spill[parity, half] = spread[pl.ds(64 + 4 * slab, 4)].astype(BF16)


def band_back(ids, band, rows):
    return pl.pallas_call(
        back_kernel,
        grid_spec=pltpu.PrefetchScalarGridSpec(
            num_scalar_prefetch=1,
            grid=(64 // GROUP,),
            in_specs=[
                pl.BlockSpec((GROUP, 256, 256), lambda i, *_: (i, 0, 0)),
                whole((64, 32, 256)),
            ],
            out_specs=[whole((80, 32, 256)), whole((2,) + PAIR)],
        ),
        out_shape=[
            jax.ShapeDtypeStruct((80, 32, 256), F32),
            jax.ShapeDtypeStruct((2,) + PAIR, BF16),
        ],
        compiler_params=params(),
        cost_estimate=pl.CostEstimate(
            flops=2 * 64 * 256 * 256 * 32, bytes_accessed=11 << 20, transcendentals=0
        ),
    )(ids, band, rows)


def far_kernel(ids, row_ids, col_ids, tiles, rows, cols, out, acc, k0, k1, k2, k3):
    mine, count = ids[0], ids[2]
    step = pl.program_id(0)

    @pl.when(step == 0)
    def _():
        out[...] = jnp.zeros_like(out)
        acc[...] = jnp.zeros_like(acc)

    def visit(base_slot, partial):
        first = step * GROUP + base_slot
        found = []
        for g in range(8):
            i = first + g
            live = i < count
            a, b = row_ids[i], col_ids[i]
            if partial:
                a, b = jnp.where(live, a, 0), jnp.where(live, b, 0)
            tile = tiles[base_slot + g]
            forward = lax.dot_general(
                cols[b], tile, (((1,), (1,)), ((), ())), preferred_element_type=F32
            )
            back = jnp.dot(rows[a], tile, preferred_element_type=F32)
            if partial:
                forward, back = jnp.where(live, forward, 0.0), jnp.where(live, back, 0.0)
            found.append((a, b, forward, back))
        for a, b, forward, back in found:
            out[a] += forward
            acc[b] += back

    for h in range(0, GROUP, 8):
        first = step * GROUP + h

        @pl.when(first + 8 <= count)
        def _():
            visit(h, False)

        @pl.when((first + 8 > count) & (first < count))
        def _():
            visit(h, True)

    @pl.when(step == pl.num_programs(0) - 1)
    def _():
        for j in range(8):
            piece = acc[pl.ds(4 * (mine ^ j), 4)]
            target = (k0, k1, k2, k3)[j & 3]
            target[j >> 2] = piece.astype(target.dtype)


def pair_shapes():
    return [jax.ShapeDtypeStruct(PAIR, F32)] + [jax.ShapeDtypeStruct(PAIR, BF16)] * 3


def far(ids, row_ids, col_ids, tiles, rows, cols):
    return pl.pallas_call(
        far_kernel,
        grid_spec=pltpu.PrefetchScalarGridSpec(
            num_scalar_prefetch=3,
            grid=(64 // GROUP,),
            in_specs=[
                pl.BlockSpec((GROUP, 256, 256), lambda i, *_: (i, 0, 0)),
                whole((64, 32, 256)),
                whole((32, 32, 256)),
            ],
            out_specs=[whole((64, 32, 256)), whole((32, 32, 256))] + [whole(PAIR)] * 4,
        ),
        out_shape=[
            jax.ShapeDtypeStruct((64, 32, 256), F32),
            jax.ShapeDtypeStruct((32, 32, 256), F32),
        ]
        + pair_shapes(),
        compiler_params=params(),
        cost_estimate=pl.CostEstimate(
            flops=4 * 64 * 256 * 256 * 32, bytes_accessed=15 << 20, transcendentals=0
        ),
    )(ids, row_ids, col_ids, tiles, rows, cols)


def forward_kernel(ids, band, rows, rim, spread, away, same, other, extended, halves):
    me = ids[1]
    step = pl.program_id(0)

    @pl.when(step == 0)
    def _():
        extended[:64] = rows[...]
        extended[64:80] = rim[...]

    first = step * GROUP
    products = [
        lax.dot_general(
            extended[first + g + me], band[g], (((1,), (1,)), ((), ())), preferred_element_type=F32
        )
        + (spread[g] + away[g])
        for g in range(GROUP)
    ]
    for h in range(GROUP // 4):
        slot = me ^ (step * (GROUP // 4) + h)
        for t in range(4):
            halves[slot & 1, slot >> 1, t] = products[4 * h + t]

    @pl.when(step == pl.num_programs(0) - 1)
    def _():
        same[...] = halves[0]
        other[...] = halves[1]


def band_forward(ids, band, rows, rim, spread, away):
    return pl.pallas_call(
        forward_kernel,
        grid_spec=pltpu.PrefetchScalarGridSpec(
            num_scalar_prefetch=1,
            grid=(64 // GROUP,),
            in_specs=[
                pl.BlockSpec((GROUP, 256, 256), lambda i, *_: (i, 0, 0)),
                whole((64, 32, 256)),
                whole((16, 32, 256)),
                pl.BlockSpec((GROUP, 32, 256), lambda i, *_: (i, 0, 0)),
                pl.BlockSpec((GROUP, 32, 256), lambda i, *_: (i, 0, 0)),
            ],
            out_specs=[whole((8, 4, 32, 256))] * 2,
            scratch_shapes=[
                pltpu.VMEM((80, 32, 256), BF16),
                pltpu.VMEM((2, 8, 4, 32, 256), F32),
            ],
        ),
        out_shape=[jax.ShapeDtypeStruct((8, 4, 32, 256), F32)] * 2,
        compiler_params=params(),
        cost_estimate=pl.CostEstimate(
            flops=0, bytes_accessed=1 << 16, transcendentals=0
        ),
    )(ids, band, rows, rim, spread, away)


def fold_kernel(ids, same, arrived, spilled, spilled_across, *outs):
    here = ids[1] >> 2
    extra = spilled[0].astype(F32) + spilled_across[...].astype(F32)
    for k in range(4):
        total = same[2 * k : 2 * k + 2] + arrived[2 * k : 2 * k + 2]
        total = total + jnp.where(here == k, extra, 0.0)
        outs[k][...] = total.astype(outs[k].dtype)


def fold(ids, same, arrived, spilled, spilled_across):
    return pl.pallas_call(
        fold_kernel,
        grid_spec=pltpu.PrefetchScalarGridSpec(
            num_scalar_prefetch=1,
            grid=(1,),
            in_specs=[whole((8, 4, 32, 256)), whole((8, 4, 32, 256)), whole((2,) + PAIR), whole(PAIR)],
            out_specs=[whole(PAIR)] * 4,
        ),
        out_shape=pair_shapes(),
        compiler_params=params(),
        cost_estimate=pl.CostEstimate(flops=0, bytes_accessed=3 << 20, transcendentals=0),
    )(ids, same, arrived, spilled, spilled_across)


def against(left, right):
    return lax.dot_general(
        left, right, (((1,), (1,)), ((), ())), precision=PRECISE, preferred_element_type=F32
    )


def image_gram_kernel(n, ids, same, other, cols, spread, *refs):
    evens, odds, alongs, rims, out = refs[:n], refs[n : 2 * n], refs[2 * n : 3 * n], refs[3 * n : 4 * n], refs[-1]

    @pl.when(pl.program_id(0) == 0)
    def _():
        out[...] = jnp.zeros_like(out)

    total = jnp.zeros((32, 32 * n), F32)
    jobs = [(same.at[0], [r.at[0] for r in evens], 4), (other.at[0], [r.at[0] for r in odds], 4)]
    jobs += [(cols, alongs, 4), (spread, rims, 2)]
    for part, known, count in jobs:
        for t in range(count):
            columns = jnp.concatenate([k[t] for k in known], axis=0)
            total += lax.dot_general(
                part[t].astype(BF16), columns, (((1,), (1,)), ((), ())), preferred_element_type=F32
            )
    out[...] += total


def image_grams(ids, same, other, cols, spread, gathered):
    n = len(gathered)
    slab = (1, 4, 32, 256)
    at_even = pl.BlockSpec(slab, lambda e, ids: (ids[1] ^ (2 * e), 0, 0, 0))
    at_odd = pl.BlockSpec(slab, lambda e, ids: (ids[1] ^ (2 * e + 1), 0, 0, 0))
    at_slab = pl.BlockSpec(slab, lambda e, ids: (e, 0, 0, 0))
    four = pl.BlockSpec((4, 32, 256), lambda e, ids: (e, 0, 0))
    two = pl.BlockSpec((2, 32, 256), lambda e, ids: (e, 0, 0))
    over = pl.BlockSpec((2, 32, 256), lambda e, ids: (32 + e, 0, 0))
    rows = [g[0].reshape(16, 4, 32, 256) for g in gathered]
    return pl.pallas_call(
        functools.partial(image_gram_kernel, n),
        grid_spec=pltpu.PrefetchScalarGridSpec(
            num_scalar_prefetch=1,
            grid=(8,),
            in_specs=[at_slab, at_slab, four, over]
            + [at_even] * n
            + [at_odd] * n
            + [four] * n
            + [two] * n,
            out_specs=whole((32, 32 * n)),
        ),
        out_shape=jax.ShapeDtypeStruct((32, 32 * n), F32),
        compiler_params=params(),
        cost_estimate=pl.CostEstimate(flops=1 << 28, bytes_accessed=8 << 20, transcendentals=0),
    )(ids, same, other, cols, spread, *rows, *rows, *[g[1] for g in gathered], *[g[2] for g in gathered])


def gram_kernel(n, *refs):
    basis, images, out = refs[: n + 1], refs[n + 1 : 2 * n + 1], refs[-1]
    total = jnp.zeros((32, 32 * (2 * n + 1)), F32)
    for t in range(4):
        columns = jnp.concatenate([b[t] for b in basis] + [b[t] for b in images], axis=0)
        total += against(basis[-1][t], columns)
    out[...] = total


def grams(older, older_images, newest):
    n = len(older)
    return pl.pallas_call(
        functools.partial(gram_kernel, n),
        out_shape=jax.ShapeDtypeStruct((32, 32 * (2 * n + 1)), F32),
        compiler_params=params(),
        cost_estimate=pl.CostEstimate(flops=1 << 27, bytes_accessed=1 << 20, transcendentals=0),
    )(*older, newest, *older_images)


def mul(left, right):
    return jnp.dot(left, right, precision=PRECISE, preferred_element_type=F32)


def mul_left(left, right):
    return lax.dot_general(
        left, right, (((0,), (0,)), ((), ())), precision=PRECISE, preferred_element_type=F32
    )


def symmetric(matrix):
    return 0.5 * (matrix + matrix.T)


def unit(order):
    return (
        lax.broadcasted_iota(jnp.int32, (order, order), 0)
        == lax.broadcasted_iota(jnp.int32, (order, order), 1)
    ).astype(F32)


def block_inverse(matrix):
    order = matrix.shape[0]
    table = jnp.concatenate([matrix, unit(order)], axis=1)
    places = lax.broadcasted_iota(jnp.int32, (order, 2 * order), 0)
    for k in range(0, order, 2):
        left = jnp.broadcast_to(table[:, k : k + 1], table.shape)
        right = jnp.broadcast_to(table[:, k + 1 : k + 2], table.shape)
        inverse = 1.0 / left[k : k + 1]
        share = right[k : k + 1] * inverse
        top = table[k : k + 1] * inverse
        corner = right[k + 1 : k + 2] - share * right[k : k + 1]
        second = (table[k + 1 : k + 2] - share * table[k : k + 1]) / corner
        table = (
            table
            - jnp.where(places > k, left, 0.0) * top
            - jnp.where(places > k + 1, right - left * share, 0.0) * second
        )
    pivots = jnp.sum(table[:, :order] * unit(order), axis=1, keepdims=True)
    return table[:, order:] * lax.rsqrt(pivots)


def factor_inverse(matrix):
    order = matrix.shape[0]
    if order == 32:
        return block_inverse(matrix)
    head = block_inverse(matrix[:32, :32])
    edge = mul(head, matrix[:32, 32:])
    rest = factor_inverse(matrix[32:, 32:] - mul_left(edge, edge))
    lower = -mul(rest, mul_left(edge, head))
    return jnp.concatenate(
        [
            jnp.concatenate([head, jnp.zeros((32, order - 32), F32)], axis=1),
            jnp.concatenate([lower, rest], axis=1),
        ],
        axis=0,
    )


def joined(top, edge, corner):
    return jnp.concatenate(
        [jnp.concatenate([top, edge.T], axis=1), jnp.concatenate([edge, corner], axis=1)], axis=0
    )


def small_start(gram):
    inverse = block_inverse(symmetric(gram[:, :32]))
    return inverse, symmetric(against(mul(inverse, symmetric(gram[:, 32:])), inverse))


def small_step(known, known_images, origin, gram, image_part, last):
    edge = known.shape[0]
    order = edge + 32
    seen = origin.shape[1]
    basis_gram = joined(known, gram[:, :edge], symmetric(gram[:, edge:order]))
    cross_images = 0.5 * (gram[:, order:] + against(image_part[:, :seen], origin))
    image_gram = joined(known_images, cross_images, symmetric(image_part[:, seen:]))
    head = lax.broadcasted_iota(jnp.int32, (1, order), 1) < 32
    down = lax.broadcasted_iota(jnp.int32, (order, 1), 0) < 32
    diagonal = basis_gram * unit(order)
    scale = jnp.where(head, 1.0, lax.rsqrt(jnp.sum(diagonal, axis=0, keepdims=True) + EPSILON))
    scale_down = jnp.where(down, 1.0, lax.rsqrt(jnp.sum(diagonal, axis=1, keepdims=True) + EPSILON))
    basis_gram = scale_down * basis_gram * scale
    image_gram = scale_down * image_gram * scale
    cross = basis_gram[32:, :32]
    tail = factor_inverse(basis_gram[32:, 32:] - against(cross, cross))
    inverse = jnp.concatenate(
        [
            jnp.concatenate([unit(32), jnp.zeros((32, edge), F32)], axis=1),
            jnp.concatenate([-mul(tail, cross), tail], axis=1),
        ],
        axis=0,
    )
    reduced = symmetric(against(mul(inverse, image_gram), inverse))
    size = jnp.sqrt(jnp.sum(jnp.sum(reduced * reduced, axis=1, keepdims=True), axis=0, keepdims=True))
    filtered = (reduced + size * unit(order)) / (2.0 * size)
    filtered = mul(filtered, filtered)
    leading = mul(filtered, filtered[:, :32])
    turned = mul(block_inverse(mul_left(leading, leading)), leading.T)
    weights = mul(turned, inverse)
    if last:
        return weights * scale, symmetric(against(mul(weights, image_gram), weights))
    weights = jnp.concatenate([weights, jnp.where(head, 0.0, weights)], axis=0)
    next_basis = symmetric(against(mul(weights, basis_gram), weights))
    next_images = symmetric(against(mul(weights, image_gram), weights))
    weights = weights * scale
    next_origin = jnp.concatenate([mul(weights[:, :edge], origin), weights[:, edge:]], axis=1)
    return weights, next_basis, next_images, next_origin


def algebra_kernel(first, last, *refs):
    if first:
        gram, weights_out, ritz_out = refs
        weights_out[...], ritz_out[...] = small_start(gram[...])
        return
    width = 2 * refs[0].shape[0] + 32
    known, known_images, origin, gram = (r[...] for r in refs[:4])
    results = small_step(known, known_images, origin, gram[:, :width], gram[:, width:], last)
    for out, value in zip(refs[4:], results):
        out[...] = value


def algebra(gram, known, last=False):
    if not known:
        shapes = [(32, 32), (32, 32)]
    elif last:
        shapes = [(32, known[0].shape[0] + 32), (32, 32)]
    else:
        shapes = [(64, known[0].shape[0] + 32), (64, 64), (64, 64), (64, known[2].shape[1] + 32)]
    return pl.pallas_call(
        functools.partial(algebra_kernel, not known, last),
        out_shape=[jax.ShapeDtypeStruct(s, F32) for s in shapes],
        compiler_params=params(),
        cost_estimate=pl.CostEstimate(flops=1 << 28, bytes_accessed=20 << 20, transcendentals=0),
    )(*known, gram)


def update_kernel(n, *refs):
    basis, images, terms = refs[:n], refs[n : 2 * n - 1], refs[2 * n - 1 : 2 * n + 3]
    mask, weights, ritz = refs[2 * n + 3], refs[2 * n + 4][...], refs[2 * n + 5][:32, :32]
    outs = refs[2 * n + 6 :]
    for t in range(4):
        newest = ((terms[0][t] + terms[1][t]) + (terms[2][t] + terms[3][t])) * mask[t]
        moved = mul(weights, jnp.concatenate([b[t] for b in basis], axis=0))
        moved_images = mul(weights, jnp.concatenate([b[t] for b in images] + [newest], axis=0))
        residual = moved_images[:32] - mul(ritz, moved[:32])
        outs[0][t] = (residual * mask[t]).astype(BF16)
        outs[1][t] = residual
        outs[2][t] = moved[:32]
        outs[3][t] = moved_images[:32]
        if n > 1:
            outs[4][t] = moved[32:]
            outs[5][t] = moved_images[32:]


def update(basis, images, terms, mask, weights, ritz):
    n = len(basis)
    slab = jax.ShapeDtypeStruct((4, 32, 256), F32)
    return pl.pallas_call(
        functools.partial(update_kernel, n),
        out_shape=[jax.ShapeDtypeStruct((4, 32, 256), BF16)] + [slab] * (3 if n == 1 else 5),
        compiler_params=params(),
        cost_estimate=pl.CostEstimate(flops=1 << 27, bytes_accessed=1 << 20, transcendentals=0),
    )(*basis, *images, *terms, mask, weights, ritz)


def finish_kernel(n, *refs):
    basis, weights, out = refs[:n], refs[n][...], refs[n + 1]
    for t in range(4):
        out[t] = mul(weights, jnp.concatenate([b[t] for b in basis], axis=0))


def finish(basis, weights):
    return pl.pallas_call(
        functools.partial(finish_kernel, len(basis)),
        out_shape=jax.ShapeDtypeStruct((4, 32, 256), F32),
        compiler_params=params(),
    )(*basis, weights)


def body(x_start, bin_mask, band, off_tiles, off_rows, off_cols, off_count):
    width = x_start.shape[1]
    band = band[:, 0]
    tiles = off_tiles[0, 0]
    row_ids, col_ids = off_rows[0, 0], off_cols[0, 0]
    ids = jnp.stack(
        [lax.axis_index("brow"), lax.axis_index("bcol"), off_count[0, 0], jnp.int32(0)]
    ).astype(jnp.int32)
    mask = bin_mask.astype(F32).reshape(4, 1, 256)
    started = x_start.T.reshape(width, 4, 256).transpose(1, 0, 2) * mask

    gathered = []

    def apply_operator(packed, plain, last=False):
        pair = jnp.stack([packed, flip(packed, "bcol", 2)])
        near = [pair] + [flip(pair, "bcol", 4 * k) for k in (1, 2, 3)]
        across = [flip(part, "bcol", 1) for part in near]
        col_pair = jnp.stack([packed, flip(packed, "brow", 4)])
        along = [col_pair] + [flip(col_pair, "brow", k) for k in (1, 2, 3)]
        rows, rim, cols = assemble(ids, near + across + along)
        spread, spill = band_back(ids, band, rows)
        if not last:
            rim, spill, spread = lax.optimization_barrier((rim, spill, spread))
            spilled = shifted(spill, "brow", 1)
        rim = shifted(rim, "brow", -1)
        gathered.append((rows, cols, rim))
        away, col_all, *col_sums = far(ids, row_ids, col_ids, tiles, rows, cols)
        same, other = band_forward(ids, band, rows, rim, spread, away)
        image_part = image_grams(ids, same, other, col_all, spread, gathered)
        gram = sum_all(jnp.concatenate([plain, image_part], axis=1))
        if last:
            return gram, None
        other, spilled = lax.optimization_barrier((other, spilled))
        arrived = flip(other, "bcol", 1)
        folded = fold(ids, same, arrived, spilled, flip(spilled[1], "bcol", 1))
        c0, c1, c2, c3 = [col_sums[0]] + [
            flip(col_sums[k], "brow", k).astype(F32) for k in (1, 2, 3)
        ]
        col_total = (c0 + c1) + (c2 + c3)
        col_other = flip(col_total[1], "brow", 4)
        r0, r1, r2, r3 = [folded[0]] + [
            flip(folded[k], "bcol", 4 * k).astype(F32) for k in (1, 2, 3)
        ]
        row_total = (r0 + r1) + (r2 + r3)
        row_other = flip(row_total[1], "bcol", 2)
        return gram, [row_total[0], row_other, col_total[0], col_other]

    gram, terms = apply_operator((started * mask).astype(BF16), grams([], [], started))
    weights, ritz = algebra(gram, [])
    known = [jnp.eye(width, dtype=F32), ritz, weights]
    packed, residual, vectors, images = update([started], [], terms, mask, weights, ritz)
    older, older_images = [vectors], [images]
    for step in range(STEPS):
        last = step == STEPS - 1
        gram, terms = apply_operator(packed, grams(older, older_images, residual), last)
        weights, *known = algebra(gram, known, last)
        basis = older + [residual]
        if not last:
            packed, residual, vectors, images, tail, tail_images = update(
                basis, older_images, terms, mask, weights, known[1]
            )
            older, older_images = [vectors, tail], [images, tail_images]
    vectors = finish(basis, weights)
    return vectors.transpose(1, 0, 2).reshape(width, -1).T, known[0]


def solution(mesh):
    return jax.shard_map(
        body,
        mesh=mesh,
        in_specs=(
            P(("brow", "bcol"), None),
            P(("brow", "bcol")),
            P("brow", "bcol", None, None),
            P("brow", "bcol", None, None, None),
            P("brow", "bcol", None),
            P("brow", "bcol", None),
            P("brow", "bcol"),
        ),
        out_specs=(P(("brow", "bcol"), None), P()),
        check_vma=False,
    )
```
